512 devices in a mesh: group: 32 (over z, y_hi, core), tp: 16 (over y_lo, x).
Axes of the slice: x: 4, y: 8 (y_hi: 2, y_lo: 4; y = y_hi * 4 + y_lo), z: 8, core: 2. Of those that a mesh axis runs over, the one named last changes fastest.
Arguments:
- hidden: bfloat16 [64, 8, 5120], P('group', None, 'tp'), may hold values from -6 to 6
- query_weight: bfloat16 [5120, 4096], P('tp'), may hold values from -0.078125 to 0.078125
- key_value_weight: bfloat16 [5120, 1024], P('tp'), may hold values from -0.078125 to 0.078125
- query_codes: bfloat16 [5120, 4096], P('tp', 'group'), may hold values from -127 to 127
- query_scales: float32 [5120, 32], P('tp', 'group'), may hold values from 2e-05 to 0.0002
- key_value_codes: bfloat16 [16, 320, 1024], P('tp', 'group'), may hold values from -127 to 127
- key_value_scales: float32 [16, 320, 8], P('tp', 'group'), may hold values from 2e-05 to 0.0002
- key_cache: bfloat16 [4, 16, 64, 16, 512], P(None, 'tp', 'group'), may hold values from -150 to 150
- value_cache: bfloat16 [4, 16, 64, 16, 512], P(None, 'tp', 'group'), may hold values from -6 to 6
- lengths: int32 [64], P('group'), may hold values from 1 to 1024
- counts: int32 [64], P('group'), may hold values from 4 to 8
- learner: int32 [64, 8, 1], P('group'), may hold values from 0 to 31; in each aligned block of 16 rows (0 to 15, 16 to 31, ..., all dimensions but the last counted through in order) at most 2 rows name the same one
- token_ids: int32 [64, 8], P('group'), may hold values from 0 to 151935
Outputs:
- trajectory_rows: bfloat16 [32, 64, 4096], P('group', None, 'tp')
- trajectory_ids: int32 [32, 64], P('group')
The draws below stay inside these ranges and needn't reach their ends.
Inputs may be any that keep to these rules, and one draw needn't show every extreme that they name: In the 16 rows of one rollout group, at most 2 name the same learner, and exactly 2 do so in some group.
All inputs are finite; a program needn't handle non-finite values.
Results may differ from the reference program's by a relative error of at most 0.012.
The reference program's roundings to bfloat16 on the way (of `query_delta`, `pair_delta`, `queries`, `pairs`, `weight` and `attended`) count: a program that leaves them out, or rounds other values in their place, can miss the bound.
Values may be sent and summed in bfloat16 or wider, within the bound.
No kernel may reach another device: no remote copies, remote signals or barrier semaphores. Data moves between devices by JAX's collectives and lax.ppermute only.
A program may use at most 64 MiB of HBM per device.

```python
import math
import jax
import jax.numpy as jnp
import numpy as np
from jax import lax

D = 5120
HEADS = 32
KV_HEADS = 4
HEAD = 128
QBLK = 128
VOCAB = 151936
STEPS = 8
BLK = 16
GAMES_G = 2
ROUNDS = 4
QW = 4096
KVW = 512
GAMES = 64
LMAX = 1024
CAP = 2
SLOTS = 64
N_GROUP = 32
N_TP = 16


def draw_key_cache(key, part):
    key = jax.random.fold_in(key, 11)
    shape = (ROUNDS, N_TP, GAMES, BLK, KV_HEADS * HEAD)
    return jnp.clip(jax.random.normal(key, shape, jnp.float32), -6.0, 6.0).astype(jnp.bfloat16)


def draw_lengths(key, part):
    key = jax.random.fold_in(key, 5)
    first, second = jax.random.split(key, 2)
    candidates = jax.random.randint(first, (3, GAMES), 1, LMAX + 1)
    shortest = jnp.min(candidates, axis=0)
    chosen = jax.random.randint(second, (), 0, GAMES)
    return shortest.at[chosen].set(LMAX).astype(jnp.int32)


def with_ends(values, rng, least, largest):
    longest = values.shape.index(max(values.shape))
    spots = []
    for shift in (0, 1):
        where = [jax.random.randint(jax.random.fold_in(rng, axis), (), 0, length) for axis, length in enumerate(values.shape)]
        where[longest] = (where[longest] + shift) % values.shape[longest]
        spots.append(tuple(where))
    return values.at[spots[0]].set(least).at[spots[1]].set(largest)


def steps_of(rng, extent, shards, least, largest):
    level = 1.0
    for dim, shards_of in shards:
        steps = jax.random.uniform(jax.random.fold_in(jax.random.fold_in(rng, 6), dim), (shards_of,), jnp.float32, least / len(shards), largest / len(shards))
        level = level * jnp.repeat(jnp.exp(steps), extent[dim] // shards_of).reshape((-1,) + (1,) * (len(extent) - 1 - dim))
    return level


def wide_ids(stream_key, shape, amount, slope):
    portions = [min(1 << octave, amount + 1 - (1 << octave)) * (1 << 20) // math.isqrt((1 << octave) ** slope) + 1 for octave in range((amount + 1).bit_length()) if 1 << octave <= amount]
    width = 1 + sum(portions) // (1 << 30)
    grid = np.cumsum(np.array([max(1, weight // width) for weight in portions]))
    ticket = jax.random.randint(jax.random.fold_in(stream_key, 1), shape, 0, int(grid[len(portions) - 1]))
    start = jnp.left_shift(1, jnp.searchsorted(jnp.asarray(grid, jnp.int32), ticket, side="right").astype(jnp.int32))
    rank = start - 1 + jax.random.randint(jax.random.fold_in(stream_key, 4), shape, 0, 1 << 30) % jnp.minimum(start, amount + 1 - start)
    return jax.random.permutation(jax.random.fold_in(stream_key, 2), amount)[rank].astype(jnp.int32)


def shared_out(own_key, own, number, rows, count, top, reach, slope):
    order = jax.random.permutation(own_key, count)
    packed, common = portions_of(count, rows * top, reach, slope, True), portions_of(count, rows * top, reach, slope, False)
    places = jnp.arange(count)

    def named(tallies, turn):
        used = int((tallies > 0).sum())
        fixed = max(1, used // 4)
        shifted = fixed + (places - fixed + turn * (used - fixed)) % max(1, count - fixed)
        return jnp.zeros((count,), jnp.int32).at[order[jnp.where(places < fixed, places, shifted)]].set(jnp.asarray(tallies, jnp.int32))

    tallies = jnp.where(number % 4 == 0, named(packed, number // 4), named(common, number - number // 4 - 1))
    mixed = jax.random.permutation(jax.random.fold_in(own, 3), count)
    donor, taker = mixed[0:count // 2 * 2:2], mixed[1:count // 2 * 2:2]
    margin = jnp.minimum(tallies[donor] - 1, reach - tallies[taker]) // 2
    margin = jnp.where((donor == order[0]) | (taker == order[0]) | (tallies[taker] == 0), 0, jnp.maximum(margin, 0))
    shifted = jax.random.randint(jax.random.fold_in(own, 4), (count // 2,), 0, 1 << 20) % (margin + 1)
    tallies = tallies.at[donor].add(-shifted).at[taker].add(shifted)
    labels = jnp.searchsorted(jnp.cumsum(tallies), jnp.arange(rows * top), side="right").astype(jnp.int32)
    listing = labels.reshape(top, rows).T
    listing = listing[jax.random.permutation(jax.random.fold_in(own, 1), rows)]
    turn = jax.random.randint(jax.random.fold_in(own, 2), (rows, 1), 0, top)
    return jnp.take_along_axis(listing, (jnp.arange(top)[None, :] + turn) % top, axis=1)


def portions_of(count, total, bound, lean, full):
    loads = [(1 << 20) // math.isqrt(grade ** lean) + 1 for grade in range(1, count + 1)]
    largest = bound if full else min(bound, max(-(-total // count), total * loads[0] // sum(loads)))
    least = 1 if total - largest >= count - 1 else 0
    holding, spare = [largest] + [least] * (count - 1), total - largest - least * (count - 1)
    while spare > 0:
        movable = [i for i in range(1, count) if holding[i] < largest] or [i for i in range(1, count) if holding[i] < bound]
        pool, budget = sum([loads[i] for i in movable]), spare
        for i in movable:
            extra = min(bound - holding[i], max(1, budget * loads[i] // pool), spare)
            holding[i] = holding[i] + extra
            spare = spare - extra
    return np.array(holding)


def bell_draw(rng, shape, spread, limit, cuts=(), held_as=jnp.bfloat16):
    loudness = steps_of(rng, shape, cuts, -0.22, 0.18) if cuts else 1.0
    values = jax.random.normal(rng, shape, jnp.float32) * spread * loudness
    return jnp.minimum(jnp.maximum(values, -limit), limit).astype(held_as)


def setup_inputs(seed: int = 0) -> dict:
    key_of = jax.random.split(jax.random.key(seed), 14)
    hidden = bell_draw(key_of[0], (GAMES, STEPS, D), 1.0, 6.0, ((0, 32), (2, 16)))
    query_weight = bell_draw(key_of[1], (D, QW), D ** -0.5, 0.078125, ((0, 16),))
    key_value_weight = bell_draw(key_of[2], (D, 2 * KVW), D ** -0.5, 0.078125, ((0, 16),))
    query_codes = bell_draw(key_of[3], (D, QW), 40.0, 127.0, ((0, 16), (1, 32)))
    query_scales = jnp.clip(jnp.exp(math.log(0.0002) - 2.3025851 * jax.random.uniform(key_of[4], (D, QW // QBLK), jnp.float32) ** steps_of(key_of[4], (D, QW // QBLK), ((0, 16), (1, 32)), -0.2, 0.2)), 1.9999999494757503e-05, 0.0002)
    key_value_codes = bell_draw(key_of[5], (N_TP, D // N_TP, 2 * KVW), 40.0, 127.0, ((0, 16), (1, 32)))
    key_value_scales = jnp.clip(jnp.exp(math.log(0.0002) - 2.3025851 * jax.random.uniform(key_of[6], (N_TP, D // N_TP, 2 * KVW // QBLK), jnp.float32) ** steps_of(key_of[6], (N_TP, D // N_TP, 2 * KVW // QBLK), ((0, 16), (1, 32)), -0.2, 0.2)), 1.9999999494757503e-05, 0.0002)
    key_cache = draw_key_cache(jax.random.fold_in(key_of[13], 71), 0)
    value_cache = bell_draw(key_of[8], (ROUNDS, N_TP, GAMES, BLK, KVW), 1.0, 6.0, ((1, 16), (2, 32)))
    lengths = draw_lengths(jax.random.fold_in(key_of[13], 71), 0)
    counts = with_ends(jax.random.randint(key_of[10], (GAMES,), STEPS // 2, STEPS + 1), jax.random.fold_in(key_of[10], 1), STEPS // 2, STEPS).astype(jnp.int32)
    learner_keys = jax.random.split(jax.random.fold_in(key_of[11], 1), GAMES * STEPS // (GAMES_G * STEPS))
    learner_turns = jax.random.permutation(jax.random.fold_in(key_of[11], 3), GAMES * STEPS // (GAMES_G * STEPS))
    learner = jax.vmap(lambda own, number: shared_out(jax.random.fold_in(key_of[11], 2), own, number, GAMES_G * STEPS, N_GROUP, 1, CAP, 1))(learner_keys, learner_turns).reshape((GAMES, STEPS, 1))
    token_ids = with_ends(wide_ids(key_of[12], (GAMES, STEPS), VOCAB, 2), jax.random.fold_in(key_of[12], 3), 0, VOCAB - 1).astype(jnp.int32)
    return dict(hidden=hidden, query_weight=query_weight, key_value_weight=key_value_weight, query_codes=query_codes, query_scales=query_scales, key_value_codes=key_value_codes, key_value_scales=key_value_scales, key_cache=key_cache, value_cache=value_cache, lengths=lengths, counts=counts, learner=learner, token_ids=token_ids)


NEG_FILL = -1e+30

def dequantize(codes, scales):
    height, columns = codes.shape
    blocks = scales.shape[-1]
    wide = codes.astype(jnp.float32).reshape(height, blocks, columns // blocks) * scales[:, :, None]
    return wide.reshape(height, columns).astype(jnp.bfloat16)

def reference(hidden, query_weight, key_value_weight, query_codes, query_scales, key_value_codes, key_value_scales, key_cache, value_cache, lengths, counts, learner, token_ids):
    members = HEADS // KV_HEADS
    token_rows = hidden.reshape(GAMES * STEPS, D)
    query_delta = dequantize(query_codes, query_scales)
    pair_delta = dequantize(key_value_codes.reshape(D, 2 * KVW), key_value_scales.reshape(D, 2 * KVW // QBLK))
    queries = jnp.dot(token_rows, query_weight, preferred_element_type=jnp.float32) + jnp.dot(token_rows, query_delta, preferred_element_type=jnp.float32)
    pairs = jnp.dot(token_rows, key_value_weight, preferred_element_type=jnp.float32) + jnp.dot(token_rows, pair_delta, preferred_element_type=jnp.float32)
    query_heads = queries.astype(jnp.bfloat16).reshape(GAMES, STEPS, KV_HEADS, members, HEAD)
    pair_heads = pairs.astype(jnp.bfloat16).reshape(GAMES, STEPS, 2, KV_HEADS, HEAD)
    key_all = jnp.transpose(key_cache, (2, 0, 1, 3, 4)).reshape(GAMES, LMAX, KV_HEADS, HEAD)
    value_all = jnp.transpose(value_cache, (2, 0, 1, 3, 4)).reshape(GAMES, LMAX, KV_HEADS, HEAD)
    factor = 1.0 / math.sqrt(HEAD)
    positions = lax.iota(jnp.int32, LMAX)
    causal = lax.iota(jnp.int32, STEPS)[None, :] <= lax.iota(jnp.int32, STEPS)[:, None]

    def one_game(items):
        query_game, pair_game, key_game, value_game, length = items
        query_float = query_game.astype(jnp.float32)
        cache_score = jnp.einsum('scrd,pcd->scrp', query_float, key_game.astype(jnp.float32)) * factor
        new_score = jnp.einsum('scrd,tcd->scrt', query_float, pair_game[:, 0].astype(jnp.float32)) * factor
        valid = (positions < length)[None, None, None, :]
        recent = causal[:, None, None, :]
        top = jnp.maximum(lax.optimization_barrier(jnp.max(jnp.where(valid, cache_score, NEG_FILL), axis=3)), lax.optimization_barrier(jnp.max(jnp.where(recent, new_score, NEG_FILL), axis=3)))
        cache_weight = jnp.where(valid, jnp.exp(cache_score - top[..., None]), 0.0).astype(jnp.bfloat16)
        new_weight = jnp.where(recent, jnp.exp(new_score - top[..., None]), 0.0).astype(jnp.bfloat16)
        total = lax.optimization_barrier(jnp.sum(cache_weight.astype(jnp.float32), axis=3)) + lax.optimization_barrier(jnp.sum(new_weight.astype(jnp.float32), axis=3))
        mixed = jnp.einsum('scrp,pcd->scrd', cache_weight.astype(jnp.float32), value_game.astype(jnp.float32))
        mixed = mixed + jnp.einsum('scrt,tcd->scrd', new_weight.astype(jnp.float32), pair_game[:, 1].astype(jnp.float32))
        return (mixed / total[..., None]).astype(jnp.bfloat16).reshape(STEPS, QW)
    attended = lax.map(one_game, (query_heads, pair_heads, key_all, value_all, lengths))
    flat_rows = attended.reshape(N_GROUP, GAMES_G * STEPS, QW)
    is_live = (lax.iota(jnp.int32, STEPS)[None, :] < counts[:, None]).reshape(N_GROUP, GAMES_G * STEPS)
    target = learner.reshape(N_GROUP, GAMES_G * STEPS)
    match = ((target[..., None] == lax.iota(jnp.int32, N_GROUP)[None, None, :]) & is_live[..., None]).astype(jnp.int32)
    earlier = jnp.cumsum(match, axis=1) - match
    order_rank = lax.optimization_barrier(jnp.sum(earlier * match, axis=2))
    slot_index = (lax.iota(jnp.int32, N_GROUP)[:, None] * CAP + order_rank).astype(jnp.int32)
    dest_row = jnp.where(is_live, target, N_GROUP).astype(jnp.int32)
    rows_out = jnp.zeros((N_GROUP, SLOTS, QW), jnp.bfloat16).at[dest_row, slot_index].set(flat_rows, mode='drop')
    ids_out = jnp.full((N_GROUP, SLOTS), -1, jnp.int32).at[dest_row, slot_index].set(token_ids.reshape(N_GROUP, GAMES_G * STEPS), mode='drop')
    return (rows_out, ids_out)
```

```python
import math

import jax
import jax.numpy as jnp
from jax import lax
from jax.sharding import PartitionSpec as P

HEADS = 32
KV_HEADS = 4
HEAD = 128
CORES = 2


NEG_FILL = -1e30


def dequantize(codes, scales):
    height, columns = codes.shape
    blocks = scales.shape[-1]
    wide = codes.astype(jnp.float32).reshape(height, blocks, columns // blocks) * scales[:, :, None]
    return wide.reshape(height, columns).astype(jnp.bfloat16)


def per_device(
    hidden,
    query_weight,
    key_value_weight,
    query_codes,
    query_scales,
    key_value_codes,
    key_value_scales,
    key_cache,
    value_cache,
    lengths,
    counts,
    learner,
    token_ids,
):
    games, steps, features = hidden.shape
    rows = games * steps
    n_group = lax.axis_size("group")
    n_tp = lax.axis_size("tp")
    chips = n_group // CORES
    group_index = lax.axis_index("group")
    chip = group_index // CORES
    core = group_index % CORES
    sharing = n_tp // KV_HEADS
    same_core = [[CORES * u + k for u in range(chips)] for k in range(CORES)]
    swap = [(g, g ^ 1) for g in range(n_group)]
    turn = [
        ((CORES * u + k) * n_tp + t, (CORES * t + k) * n_tp + u)
        for u in range(chips)
        for k in range(CORES)
        for t in range(n_tp)
    ]
    wide = HEADS // n_tp * HEAD
    pair_rows = key_value_codes.shape[1]

    query_mine = dequantize(query_codes, query_scales)
    query_other = lax.ppermute(query_mine, "group", swap)

    rounds, _, _, block, _ = key_cache.shape
    both = jnp.stack([key_cache, value_cache]).reshape(2, rounds, games, block, KV_HEADS, HEAD)
    both = jnp.transpose(both, (4, 0, 1, 2, 3, 5))
    both = jnp.broadcast_to(both[:, None], (KV_HEADS, sharing) + both.shape[1:])
    both = both.reshape((n_tp,) + both.shape[2:])
    cache = lax.all_to_all(both, "tp", split_axis=0, concat_axis=0, tiled=True)

    pair_mine = dequantize(key_value_codes[0], key_value_scales[0])
    pair_heads = pair_mine.reshape(pair_rows, 2, KV_HEADS, HEAD).transpose(2, 0, 1, 3)
    pair_heads = pair_heads.reshape(KV_HEADS, pair_rows, 2 * HEAD)
    is_live = (lax.iota(jnp.int32, steps)[None, :] < counts[:, None]).reshape(rows)
    target = jnp.where(is_live, learner.reshape(rows), -1)
    flat_ids = token_ids.reshape(rows)
    facts = jnp.stack([flat_ids // 4096, flat_ids // 64 % 64, flat_ids % 64, target])
    facts = facts.astype(jnp.bfloat16)
    x_part = jnp.pad(hidden.reshape(rows, features), ((0, 0), (0, 64)))
    facts_part = jnp.pad(facts, ((0, pair_rows - 4), (0, 128 - rows)))
    pair_part = jnp.concatenate(
        [pair_heads, jnp.broadcast_to(facts_part, (KV_HEADS,) + facts_part.shape)], axis=2
    )
    pair_part = jnp.pad(pair_part, ((0, 0), (0, 16 - pair_rows), (0, 0)))
    load = jnp.concatenate([jnp.broadcast_to(x_part, (KV_HEADS,) + x_part.shape), pair_part], axis=1)
    load = jnp.broadcast_to(load[:, None], (KV_HEADS, chips // KV_HEADS) + load.shape[1:])
    load = load.reshape((chips,) + load.shape[2:])
    came = lax.all_to_all(
        load, "group", split_axis=0, concat_axis=0, tiled=True, axis_index_groups=same_core
    )
    x_all = came[:, :rows, :features].reshape(chips * rows, features)
    delta_mine = came[:, rows:]
    delta_other = lax.ppermute(delta_mine, "group", swap)
    delta = jnp.stack([delta_mine, delta_other])

    query_delta = jnp.where(
        core == 0,
        jnp.concatenate([query_mine, query_other], axis=1),
        jnp.concatenate([query_other, query_mine], axis=1),
    )
    head = chip // (chips // KV_HEADS)
    query_base = lax.dynamic_slice_in_dim(query_weight, chip * wide, wide, 1)
    pair_base = jnp.concatenate(
        [
            lax.dynamic_slice_in_dim(key_value_weight, head * HEAD, HEAD, 1),
            lax.dynamic_slice_in_dim(key_value_weight, (KV_HEADS + head) * HEAD, HEAD, 1),
        ],
        axis=1,
    )
    spot = lax.iota(jnp.int32, CORES * chips * 16)
    owner = spot // 16 % chips * CORES + (spot // 16 // chips + core) % 2
    source = jnp.where(spot % 16 < pair_rows, owner * pair_rows + spot % 16, -1)
    spread = (lax.iota(jnp.int32, features)[:, None] == source[None, :]).astype(jnp.bfloat16)
    x_spread = jnp.dot(x_all, spread, preferred_element_type=jnp.float32).astype(jnp.bfloat16)
    pair_delta = delta[..., : 2 * HEAD].reshape(CORES * chips * 16, 2 * HEAD)
    query_part = jnp.dot(x_all, query_base, preferred_element_type=jnp.float32) + jnp.dot(
        x_all, query_delta, preferred_element_type=jnp.float32
    )
    pair_part = jnp.dot(x_all, pair_base, preferred_element_type=jnp.float32) + jnp.dot(
        x_spread, pair_delta, preferred_element_type=jnp.float32
    )
    part = jnp.concatenate([query_part, pair_part], axis=1).reshape(chips, rows, wide + 2 * HEAD)
    parts = lax.all_to_all(part, "tp", split_axis=0, concat_axis=0, tiled=True)
    mine = jnp.sum(parts, axis=0).astype(jnp.bfloat16)
    mine = lax.ppermute(mine, ("group", "tp"), turn)

    all_facts = delta[:, :, :4, 2 * HEAD : 2 * HEAD + rows].astype(jnp.int32)
    all_facts = jnp.where(core == 0, all_facts, all_facts[::-1])
    all_facts = all_facts.transpose(2, 1, 0, 3).reshape(4, n_group, rows)
    all_ids = all_facts[0] * 4096 + all_facts[1] * 64 + all_facts[2]
    hits = all_facts[3] == group_index
    hit_rank = jnp.cumsum(hits.astype(jnp.int32), axis=1) - 1
    capacity = max(2, 2 * rows // n_group)
    chosen = hits[:, None, :] & (hit_rank[:, None, :] == lax.iota(jnp.int32, capacity)[None, :, None])
    ids_back = jnp.where(
        jnp.any(chosen, axis=2), jnp.sum(jnp.where(chosen, all_ids[:, None, :], 0), axis=2), -1
    ).reshape(1, n_group * capacity)

    per = HEADS // n_tp
    queries = mine[:, :wide].reshape(games, steps, per, HEAD)
    new_keys = mine[:, wide : wide + HEAD].reshape(games, steps, HEAD)
    new_values = mine[:, wide + HEAD :].reshape(games, steps, HEAD)
    key_rows = cache[:, 0]
    value_rows = cache[:, 1]
    factor = 1.0 / math.sqrt(HEAD)
    scores = (
        jnp.einsum("gshd,trgbd->gshtrb", queries, key_rows, preferred_element_type=jnp.float32)
        * factor
    )
    position = (
        (lax.iota(jnp.int32, rounds)[None, :, None] * n_tp + lax.iota(jnp.int32, n_tp)[:, None, None])
        * block
        + lax.iota(jnp.int32, block)[None, None, :]
    )
    valid = (position[None] < lengths[:, None, None, None])[:, None, None]
    new_scores = (
        jnp.einsum("gshd,gjd->gshj", queries, new_keys, preferred_element_type=jnp.float32) * factor
    )
    causal = lax.iota(jnp.int32, steps)[None, :] <= lax.iota(jnp.int32, steps)[:, None]
    new_valid = causal[None, :, None, :]
    top = jnp.maximum(
        jnp.max(jnp.where(valid, scores, NEG_FILL), axis=(3, 4, 5)),
        jnp.max(jnp.where(new_valid, new_scores, NEG_FILL), axis=3),
    )
    weight = jnp.where(valid, jnp.exp(scores - top[..., None, None, None]), 0.0).astype(jnp.bfloat16)
    new_weight = jnp.where(new_valid, jnp.exp(new_scores - top[..., None]), 0.0).astype(jnp.bfloat16)
    total = jnp.sum(weight.astype(jnp.float32), axis=(3, 4, 5)) + jnp.sum(
        new_weight.astype(jnp.float32), axis=3
    )
    mixed = jnp.einsum(
        "gshtrb,trgbd->gshd", weight, value_rows, preferred_element_type=jnp.float32
    ) + jnp.einsum("gshj,gjd->gshd", new_weight, new_values, preferred_element_type=jnp.float32)
    attended = (mixed / total[..., None]).astype(jnp.bfloat16).reshape(rows, wide)

    match = (target[:, None] == lax.iota(jnp.int32, n_group)[None, :]).astype(jnp.int32)
    earlier = jnp.cumsum(match, axis=0) - match
    order_rank = jnp.sum(earlier * match, axis=1)
    slot_index = jnp.where(is_live, target * capacity + order_rank, -1)
    placed = lax.iota(jnp.int32, n_group * capacity)[:, None] == slot_index[None, :]
    packed = jnp.dot(
        placed.astype(jnp.bfloat16), attended, preferred_element_type=jnp.float32
    ).astype(jnp.bfloat16)
    packed = packed.reshape(n_group, capacity, wide)
    rows_back = lax.all_to_all(packed, "group", split_axis=0, concat_axis=1, tiled=True)
    return (rows_back, ids_back)


def solution(mesh):
    placed = (
        P("group", None, "tp"),
        P("tp", None),
        P("tp", None),
        P("tp", "group"),
        P("tp", "group"),
        P("tp", "group", None),
        P("tp", "group", None),
        P(None, "tp", "group", None, None),
        P(None, "tp", "group", None, None),
        P("group"),
        P("group"),
        P("group", None, None),
        P("group", None),
    )
    return jax.shard_map(
        per_device,
        mesh=mesh,
        in_specs=placed,
        out_specs=(P("group", None, "tp"), P("group", None)),
        check_vma=False,
    )
```

```python
import functools
import math

import jax
import jax.numpy as jnp
from jax import lax
from jax.experimental import pallas as pl
from jax.experimental.pallas import tpu as pltpu
from jax.sharding import PartitionSpec as P

HEADS = 32
KV_HEADS = 4
HEAD = 128
CORES = 2
TILE = 16
LANES = 128


NEG_FILL = -1e30

VMEM = pl.BlockSpec(memory_space=pltpu.VMEM)
SMEM = pl.BlockSpec(memory_space=pltpu.SMEM)
PARAMS = pltpu.CompilerParams(vmem_limit_bytes=32 * 1024 * 1024)


def column(row):
    n = row.shape[1]
    across = lax.broadcasted_iota(jnp.int32, (n, n), 1)
    down = lax.broadcasted_iota(jnp.int32, (n, n), 0)
    return jnp.sum(jnp.where(across == down, row, jnp.zeros_like(row)), axis=1, keepdims=True)


def load_kernel(counts_ref, hidden_ref, codes_ref, scales_ref, learner_ref, ids_ref, load_ref):
    chips = load_ref.shape[0]
    rows, features = hidden_ref.shape
    pair_rows = codes_ref.shape[0]
    games, steps = ids_ref.shape
    load_ref[...] = jnp.zeros_like(load_ref)
    load_ref[:, :rows, :features] = jnp.broadcast_to(hidden_ref[...], (chips, rows, features))
    per_head = chips // KV_HEADS
    for block in range(2 * KV_HEADS):
        scale = column(scales_ref[block : block + 1, :])
        codes = codes_ref[:, block * HEAD : (block + 1) * HEAD].astype(jnp.float32)
        delta = (codes * scale).astype(jnp.bfloat16)
        head, part = block % KV_HEADS, block // KV_HEADS
        load_ref[
            head * per_head : (head + 1) * per_head,
            rows : rows + pair_rows,
            part * HEAD : (part + 1) * HEAD,
        ] = jnp.broadcast_to(delta, (per_head, pair_rows, HEAD))
    step = lax.broadcasted_iota(jnp.int32, (1, steps), 1)
    ids = ids_ref[...]
    named = [
        jnp.where(step < counts_ref[game], learner_ref[game], -1) for game in range(games)
    ]
    facts = jnp.concatenate([ids >> 12, (ids >> 6) & 63, ids & 63] + named, axis=0)
    facts = facts.astype(jnp.float32).astype(jnp.bfloat16)
    load_ref[:, rows : rows + 4 * games, 2 * HEAD : 2 * HEAD + steps] = jnp.broadcast_to(
        facts, (chips,) + facts.shape
    )


def pieces_kernel(place_ref, codes_ref, scales_ref, key_ref, value_ref, delta_ref, *piece_refs):
    scale = column(scales_ref[...])
    delta_ref[...] = (codes_ref[...].astype(jnp.float32) * scale).astype(jnp.bfloat16)
    for shift, piece_ref in enumerate(piece_refs):
        head = lax.rem(place_ref[0] + shift, KV_HEADS)
        lanes = pl.ds(pl.multiple_of(head * HEAD, HEAD), HEAD)
        piece_ref[0] = key_ref[:, 0, :, :, lanes]
        piece_ref[1] = value_ref[:, 0, :, :, lanes]


def part_kernel(
    place_ref,
    came_ref,
    other_ref,
    delta_mine_ref,
    delta_other_ref,
    query_ref,
    key_ref,
    value_ref,
    piece0_ref,
    piece1_ref,
    piece2_ref,
    piece3_ref,
    part_ref,
    shard_ref,
):
    chips, rows = part_ref.shape[:2]
    features = query_ref.shape[0]
    wide = query_ref.shape[1]
    core = place_ref[2]
    pair_rows = features // (chips * CORES)

    def dot(a, b):
        return jnp.dot(a, b, preferred_element_type=jnp.float32)

    inputs = came_ref[:, :rows, :features].reshape(chips * rows, features)
    mine, other = delta_mine_ref[...], delta_other_ref[...]
    first = jnp.where(core == 0, mine, other)
    second = jnp.where(core == 0, other, mine)
    queries = dot(inputs, query_ref[...])
    part_ref[:, :, :HEAD] = (queries[:, :HEAD] + dot(inputs, first)).reshape(chips, rows, HEAD)
    part_ref[:, :, HEAD:wide] = (queries[:, HEAD:] + dot(inputs, second)).reshape(chips, rows, HEAD)
    spot = lax.broadcasted_iota(jnp.int32, (1, chips * TILE), 1)
    feature = lax.broadcasted_iota(jnp.int32, (features, chips * TILE), 0)
    pairs = jnp.zeros((chips * rows, 2 * HEAD), jnp.float32)
    for turn, delta_ref in enumerate((came_ref, other_ref)):
        owner = (spot // TILE) * CORES + (core + turn) % CORES
        source = jnp.where(spot % TILE < pair_rows, owner * pair_rows + spot % TILE, -1)
        spread = (feature == source).astype(jnp.float32).astype(jnp.bfloat16)
        spread = dot(inputs, spread).astype(jnp.bfloat16)
        delta = delta_ref[:, rows:, : 2 * HEAD] if turn == 0 else delta_ref[:, :, : 2 * HEAD]
        pairs = pairs + dot(spread, delta.reshape(chips * TILE, 2 * HEAD))
    part_ref[:, :, wide : wide + HEAD] = (pairs[:, :HEAD] + dot(inputs, key_ref[...])).reshape(
        chips, rows, HEAD
    )
    part_ref[:, :, wide + HEAD :] = (pairs[:, HEAD:] + dot(inputs, value_ref[...])).reshape(
        chips, rows, HEAD
    )
    for shift, piece_ref in enumerate((piece0_ref, piece1_ref, piece2_ref, piece3_ref)):
        shard_ref[shift] = piece_ref[...]


def attend_kernel(
    place_ref,
    lengths_ref,
    mine_ref,
    placed_ref,
    shard0_ref,
    shard1_ref,
    shard2_ref,
    shard3_ref,
    packed_ref,
):
    shards = (shard0_ref, shard1_ref, shard2_ref, shard3_ref)
    count, _, rounds, games, block, _ = shard0_ref.shape
    rows = mine_ref.shape[0]
    steps = rows // games
    heads = mine_ref.shape[1] // HEAD - 2
    n_tp = count * len(shards)
    factor = 1.0 / math.sqrt(HEAD)
    mine = mine_ref[...].astype(jnp.float32)
    spot = lax.broadcasted_iota(jnp.int32, (1, count * rounds * block), 1)
    positions = []
    for shift in range(len(shards)):
        across = lax.rem(place_ref[1] - shift + len(shards), len(shards))
        down = (place_ref[0] - spot // (rounds * block) + count) % count
        tp = down * len(shards) + across
        positions.append((spot // block % rounds * n_tp + tp) * block + spot % block)
    contract = (((1,), (1,)), ((), ()))
    games_out = []
    for game in range(games):
        band = mine[game * steps : (game + 1) * steps]
        queries = jnp.concatenate(
            [band[:, h * HEAD : (h + 1) * HEAD] for h in range(heads)], axis=0
        ).astype(jnp.bfloat16)
        new_keys = band[:, heads * HEAD : (heads + 1) * HEAD].astype(jnp.bfloat16)
        new_values = band[:, (heads + 1) * HEAD :].astype(jnp.bfloat16)
        new_scores = factor * lax.dot_general(
            queries, new_keys, contract, preferred_element_type=jnp.float32
        )
        later = lax.broadcasted_iota(jnp.int32, new_scores.shape, 1)
        step = lax.broadcasted_iota(jnp.int32, new_scores.shape, 0) % steps
        new_valid = later <= step
        top = jnp.max(jnp.where(new_valid, new_scores, NEG_FILL), axis=1, keepdims=True)
        kept = []
        for shard_ref, position in zip(shards, positions):
            keys = shard_ref[:, 0, :, game].reshape(count * rounds * block, HEAD)
            scores = factor * lax.dot_general(
                queries, keys, contract, preferred_element_type=jnp.float32
            )
            scores = jnp.where(position < lengths_ref[game], scores, NEG_FILL)
            top = jnp.maximum(top, jnp.max(scores, axis=1, keepdims=True))
            kept.append(scores)
        weight = jnp.where(new_valid, jnp.exp(new_scores - top), 0.0).astype(jnp.bfloat16)
        total = jnp.sum(weight.astype(jnp.float32), axis=1, keepdims=True)
        mixed = jnp.dot(weight, new_values, preferred_element_type=jnp.float32)
        for shard_ref, position, scores in zip(shards, positions, kept):
            values = shard_ref[:, 1, :, game].reshape(count * rounds * block, HEAD)
            weight = jnp.where(
                position < lengths_ref[game], jnp.exp(scores - top), 0.0
            ).astype(jnp.bfloat16)
            total = total + jnp.sum(weight.astype(jnp.float32), axis=1, keepdims=True)
            mixed = mixed + jnp.dot(weight, values, preferred_element_type=jnp.float32)
        out = mixed / total
        games_out.append(
            jnp.concatenate([out[h * steps : (h + 1) * steps] for h in range(heads)], axis=1)
        )
    attended = jnp.concatenate(games_out, axis=0).astype(jnp.bfloat16)
    packed_ref[...] = jnp.dot(
        placed_ref[...], attended, preferred_element_type=jnp.float32
    ).astype(jnp.bfloat16)


def places(counts, learner, n_group, capacity):
    games, steps, _ = learner.shape
    rows = games * steps
    is_live = (lax.iota(jnp.int32, steps)[None, :] < counts[:, None]).reshape(rows)
    target = jnp.where(is_live, learner.reshape(rows), -1)
    match = (target[:, None] == lax.iota(jnp.int32, n_group)[None, :]).astype(jnp.int32)
    earlier = jnp.cumsum(match, axis=0) - match
    order_rank = jnp.sum(earlier * match, axis=1)
    slot_index = jnp.where(is_live, target * capacity + order_rank, -1)
    placed = lax.iota(jnp.int32, n_group * capacity)[:, None] == slot_index[None, :]
    return placed.astype(jnp.bfloat16)


def ids_of(facts, group_index, capacity):
    n_group, kinds, rows = facts.shape[0], 4, facts.shape[1] * facts.shape[2] // 4
    facts = facts.reshape(n_group, kinds, rows).astype(jnp.int32)
    all_ids = facts[:, 0] * 4096 + facts[:, 1] * 64 + facts[:, 2]
    hits = facts[:, 3] == group_index
    hit_rank = jnp.cumsum(hits.astype(jnp.int32), axis=1) - 1
    chosen = hits[:, None, :] & (hit_rank[:, None, :] == lax.iota(jnp.int32, capacity)[None, :, None])
    found = jnp.sum(jnp.where(chosen, all_ids[:, None, :], 0), axis=2)
    return jnp.where(jnp.any(chosen, axis=2), found, -1).reshape(1, n_group * capacity)


def per_device(
    hidden,
    query_weight,
    key_value_weight,
    query_codes,
    query_scales,
    key_value_codes,
    key_value_scales,
    key_cache,
    value_cache,
    lengths,
    counts,
    learner,
    token_ids,
):
    games, steps, features = hidden.shape
    rows = games * steps
    n_group = lax.axis_size("group")
    n_tp = lax.axis_size("tp")
    chips = n_group // CORES
    group_index = lax.axis_index("group")
    tp_index = lax.axis_index("tp")
    chip = group_index // CORES
    core = group_index % CORES
    across = n_tp // KV_HEADS
    same_core = [[CORES * u + k for u in range(chips)] for k in range(CORES)]
    swap = [(g, g ^ 1) for g in range(n_group)]
    turn = [
        ((CORES * u + k) * n_tp + t, (CORES * t + k) * n_tp + u)
        for u in range(chips)
        for k in range(CORES)
        for t in range(n_tp)
    ]
    wide = HEADS // n_tp * HEAD
    capacity = max(2, 2 * rows // n_group)
    rounds, _, _, block, _ = key_cache.shape
    head = chip // (chips // KV_HEADS)
    place = jnp.stack([tp_index // across, tp_index % across, core, chip, head]).astype(jnp.int32)

    load = pl.pallas_call(
        load_kernel,
        out_shape=jax.ShapeDtypeStruct((chips, 2 * TILE, 3 * LANES), jnp.bfloat16),
        in_specs=[SMEM] + [VMEM] * 5,
        out_specs=VMEM,
        compiler_params=PARAMS,
        name="load",
    )(
        counts,
        hidden.reshape(rows, features),
        key_value_codes[0],
        key_value_scales[0].T,
        learner.transpose(0, 2, 1),
        token_ids,
    )
    came = lax.all_to_all(
        load, "group", split_axis=0, concat_axis=0, tiled=True, axis_index_groups=same_core
    )

    piece = jax.ShapeDtypeStruct((2, rounds, games, block, HEAD), jnp.bfloat16)
    query_mine, *pieces = pl.pallas_call(
        pieces_kernel,
        out_shape=[jax.ShapeDtypeStruct(query_codes.shape, jnp.bfloat16)] + [piece] * KV_HEADS,
        in_specs=[SMEM] + [VMEM] * 4,
        out_specs=[VMEM] * (1 + KV_HEADS),
        compiler_params=PARAMS,
        name="pieces",
    )(place, query_codes, query_scales.T, key_cache, value_cache)
    query_other = lax.ppermute(query_mine, "group", swap)
    for shift in range(1, KV_HEADS):
        pairs = [(t, (t + shift * across) % n_tp) for t in range(n_tp)]
        pieces[shift] = lax.ppermute(pieces[shift], "tp", pairs)
    delta_mine = came[:, rows:]
    delta_other = lax.ppermute(delta_mine, "group", swap)

    part, shard = pl.pallas_call(
        part_kernel,
        grid_spec=pltpu.PrefetchScalarGridSpec(
            num_scalar_prefetch=1,
            grid=(1,),
            in_specs=[VMEM] * 4
            + [
                pl.BlockSpec((features, wide), lambda i, place: (0, place[3])),
                pl.BlockSpec((features, HEAD), lambda i, place: (0, place[4])),
                pl.BlockSpec((features, HEAD), lambda i, place: (0, KV_HEADS + place[4])),
            ]
            + [VMEM] * 4,
            out_specs=[VMEM] * 2,
        ),
        out_shape=[
            jax.ShapeDtypeStruct((chips, rows, wide + 2 * HEAD), jnp.float32),
            jax.ShapeDtypeStruct((KV_HEADS,) + piece.shape, jnp.bfloat16),
        ],
        compiler_params=PARAMS,
        name="part",
    )(
        place,
        came,
        delta_other,
        query_mine,
        query_other,
        query_weight,
        key_value_weight,
        key_value_weight,
        *pieces,
    )
    parts = lax.all_to_all(part, "tp", split_axis=0, concat_axis=0, tiled=True)
    shards = [shard]
    for shift in range(1, across):
        pairs = [(t, t // across * across + (t + shift) % across) for t in range(n_tp)]
        shards.append(lax.ppermute(shard, "tp", pairs))
    mine = jnp.sum(parts, axis=0).astype(jnp.bfloat16)
    mine = lax.ppermute(mine, ("group", "tp"), turn)

    packed = pl.pallas_call(
        attend_kernel,
        out_shape=jax.ShapeDtypeStruct((n_group * capacity, wide), jnp.bfloat16),
        in_specs=[SMEM, SMEM] + [VMEM] * 6,
        out_specs=VMEM,
        compiler_params=PARAMS,
        name="attend",
    )(place, lengths, mine, places(counts, learner, n_group, capacity), *shards)
    packed = packed.reshape(n_group, capacity, wide)
    rows_back = lax.all_to_all(packed, "group", split_axis=0, concat_axis=1, tiled=True)

    both = jnp.stack([delta_mine, delta_other])[:, :, : 4 * games, 2 * HEAD : 2 * HEAD + steps]
    both = jnp.where(core == 0, both, both[::-1]).transpose(1, 0, 2, 3)
    ids_back = ids_of(both.reshape(n_group, 4 * games, steps), group_index, capacity)
    return (rows_back, ids_back)


def solution(mesh):
    placed = (
        P("group", None, "tp"),
        P("tp", None),
        P("tp", None),
        P("tp", "group"),
        P("tp", "group"),
        P("tp", "group", None),
        P("tp", "group", None),
        P(None, "tp", "group", None, None),
        P(None, "tp", "group", None, None),
        P("group"),
        P("group"),
        P("group", None, None),
        P("group", None),
    )
    return jax.shard_map(
        per_device,
        mesh=mesh,
        in_specs=placed,
        out_specs=(P("group", None, "tp"), P("group", None)),
        check_vma=False,
    )
```

```python
import math

import jax
import jax.numpy as jnp
from jax import lax
from jax.experimental import pallas as pl
from jax.experimental.pallas import tpu as pltpu
from jax.sharding import PartitionSpec as P

HEADS = 32
KV_HEADS = 4
HEAD = 128
CORES = 2
TILE = 16
LANES = 128


NEG_FILL = -1e30

VMEM = pl.BlockSpec(memory_space=pltpu.VMEM)
SMEM = pl.BlockSpec(memory_space=pltpu.SMEM)
HBM = pl.BlockSpec(memory_space=pltpu.HBM)
ANY = pl.BlockSpec(memory_space=pl.ANY)
PARAMS = pltpu.CompilerParams(vmem_limit_bytes=24 * 1024 * 1024)


def column(row):
    n = row.shape[1]
    across = lax.broadcasted_iota(jnp.int32, (n, n), 1)
    down = lax.broadcasted_iota(jnp.int32, (n, n), 0)
    return jnp.sum(jnp.where(across == down, row, jnp.zeros_like(row)), axis=1, keepdims=True)


def fetch(pairs, sems):
    copies = [
        pltpu.make_async_copy(source, target, sems.at[i]) for i, (source, target) in enumerate(pairs)
    ]
    for copy in copies:
        copy.start()
    return copies


def load_kernel(
    counts_hbm,
    hidden_hbm,
    codes_hbm,
    scales_hbm,
    learner_hbm,
    ids_hbm,
    load_ref,
    named_ref,
    counts_ref,
    hidden_ref,
    codes_ref,
    scales_ref,
    learner_ref,
    ids_ref,
    sems,
):
    copies = fetch(
        [
            (codes_hbm, codes_ref),
            (scales_hbm, scales_ref),
            (hidden_hbm, hidden_ref),
            (counts_hbm, counts_ref),
            (learner_hbm, learner_ref),
            (ids_hbm, ids_ref),
        ],
        sems,
    )
    chips = load_ref.shape[0]
    rows, features = hidden_ref.shape
    pair_rows = codes_ref.shape[0]
    games, steps = ids_ref.shape
    load_ref[...] = jnp.zeros_like(load_ref)
    for copy in copies:
        copy.wait()
    load_ref[:, :rows, :features] = jnp.broadcast_to(hidden_ref[...], (chips, rows, features))
    per_head = chips // KV_HEADS
    for block in range(2 * KV_HEADS):
        scale = column(scales_ref[block : block + 1, :])
        codes = codes_ref[:, block * HEAD : (block + 1) * HEAD].astype(jnp.float32)
        delta = (codes * scale).astype(jnp.bfloat16)
        head, part = block % KV_HEADS, block // KV_HEADS
        load_ref[
            head * per_head : (head + 1) * per_head,
            rows : rows + pair_rows,
            part * HEAD : (part + 1) * HEAD,
        ] = jnp.broadcast_to(delta, (per_head, pair_rows, HEAD))
    step = lax.broadcasted_iota(jnp.int32, (1, steps), 1)
    ids = ids_ref[...]
    named = [
        jnp.where(step < counts_ref[game], learner_ref[game], -1) for game in range(games)
    ]
    named_ref[...] = jnp.concatenate(named, axis=1)
    facts = jnp.concatenate([ids >> 12, (ids >> 6) & 63, ids & 63] + named, axis=0)
    facts = facts.astype(jnp.float32).astype(jnp.bfloat16)
    load_ref[:, rows : rows + 4 * games, 2 * HEAD : 2 * HEAD + steps] = jnp.broadcast_to(
        facts, (chips,) + facts.shape
    )


def pieces_kernel(
    codes_hbm,
    scales_hbm,
    key_hbm,
    value_hbm,
    delta_ref,
    piece0_ref,
    piece1_ref,
    piece2_ref,
    piece3_ref,
    codes_ref,
    scales_ref,
    sems,
    piece_sems,
):
    copies = fetch([(codes_hbm, codes_ref), (scales_hbm, scales_ref)], sems)
    own = lax.axis_index("tp") // (lax.axis_size("tp") // KV_HEADS)
    moves = []
    for shift, piece_ref in enumerate((piece0_ref, piece1_ref, piece2_ref, piece3_ref)):
        head = lax.rem(own + shift, KV_HEADS)
        lanes = pl.ds(pl.multiple_of(head * HEAD, HEAD), HEAD)
        for part, cache_hbm in enumerate((key_hbm, value_hbm)):
            moves.append((cache_hbm.at[:, 0, :, :, lanes], piece_ref.at[part]))
    moves = fetch(moves, piece_sems)
    for copy in copies:
        copy.wait()
    scale = column(scales_ref[...])
    delta_ref[...] = (codes_ref[...].astype(jnp.float32) * scale).astype(jnp.bfloat16)
    for copy in moves:
        copy.wait()


def swap_kernel(came_ref, query_ref, after1_ref, after2_ref, after3_ref, out_ref):
    chips, depth, width = came_ref.shape
    block = chips * TILE
    for i in range(width // LANES):
        out_ref[i * block : (i + 1) * block] = came_ref[
            :, depth - TILE :, i * LANES : (i + 1) * LANES
        ].reshape(block, LANES)
    out_ref[width // LANES * block :] = query_ref[...]


def part_kernel(
    came_ref,
    other_ref,
    delta_ref,
    query_hbm,
    pair_hbm,
    part_ref,
    query_ref,
    key_ref,
    value_ref,
    sems,
):
    chips, rows = part_ref.shape[:2]
    features, wide = query_ref.shape
    block = chips * TILE
    group_index = lax.axis_index("group")
    chip, core = group_index // CORES, lax.rem(group_index, CORES)
    head = chip // (chips // KV_HEADS)
    pair_rows = features // (chips * CORES)

    def columns(source, start, size):
        return source.at[:, pl.ds(pl.multiple_of(start, HEAD), size)]

    copies = fetch(
        [
            (columns(query_hbm, chip * wide, wide), query_ref),
            (columns(pair_hbm, head * HEAD, HEAD), key_ref),
            (columns(pair_hbm, (KV_HEADS + head) * HEAD, HEAD), value_ref),
        ],
        sems,
    )

    def dot(a, b):
        return jnp.dot(a, b, preferred_element_type=jnp.float32)

    inputs = came_ref[:, :rows, :features].reshape(block, features)
    spot = lax.broadcasted_iota(jnp.int32, (1, block), 1)
    feature = lax.broadcasted_iota(jnp.int32, (features, block), 0)
    keys = jnp.zeros((block, HEAD), jnp.float32)
    values = jnp.zeros((block, HEAD), jnp.float32)
    for turn in range(CORES):
        owner = (spot // TILE) * CORES + lax.rem(core + turn, CORES)
        source = jnp.where(spot % TILE < pair_rows, owner * pair_rows + spot % TILE, -1)
        spread = (feature == source).astype(jnp.float32).astype(jnp.bfloat16)
        spread = dot(inputs, spread).astype(jnp.bfloat16)
        if turn == 0:
            key_delta = came_ref[:, rows:, :HEAD].reshape(block, HEAD)
            value_delta = came_ref[:, rows:, HEAD : 2 * HEAD].reshape(block, HEAD)
        else:
            key_delta = other_ref[:block]
            value_delta = other_ref[block : 2 * block]
        keys = keys + dot(spread, key_delta)
        values = values + dot(spread, value_delta)
    mine, other = delta_ref[...], other_ref[3 * block :]
    first = dot(inputs, jnp.where(core == 0, mine, other))
    second = dot(inputs, jnp.where(core == 0, other, mine))
    for copy in copies:
        copy.wait()
    queries = dot(inputs, query_ref[...])

    def put(i, sums):
        part_ref[:, :, i * HEAD : (i + 1) * HEAD] = sums.reshape(chips, rows, HEAD)

    put(0, queries[:, :HEAD] + first)
    put(1, queries[:, HEAD:] + second)
    put(2, keys + dot(inputs, key_ref[...]))
    put(3, values + dot(inputs, value_ref[...]))


def join_kernel(after_ref, *refs):
    shard_ref = refs[-1]
    for shift, piece_ref in enumerate(refs[:-1]):
        shard_ref[shift] = piece_ref[...]


def facts_kernel(after_ref, named_ref, came_ref, other_ref, placed_ref, ids_ref):
    chips, depth, _ = came_ref.shape
    block = chips * TILE
    slots, rows = placed_ref.shape
    steps = rows // 2
    group_index = lax.axis_index("group")
    core = lax.rem(group_index, CORES)
    capacity = slots // (chips * CORES)

    named = named_ref[...].astype(jnp.float32)
    before = lax.broadcasted_iota(jnp.int32, (rows, rows), 0) < lax.broadcasted_iota(
        jnp.int32, (rows, rows), 1
    )
    rank = jnp.sum(jnp.where((column(named) == named) & before, 1.0, 0.0), axis=0, keepdims=True)
    slot = jnp.where(named >= 0, named * capacity + rank, -1.0)
    index = lax.broadcasted_iota(jnp.int32, (slots, rows), 0).astype(jnp.float32)
    placed_ref[...] = jnp.where(index == slot, 1.0, 0.0).astype(jnp.bfloat16)

    own = came_ref[:, depth - TILE :, 2 * HEAD :].astype(jnp.float32)
    other = other_ref[2 * block : 3 * block].reshape(own.shape).astype(jnp.float32)
    kind = lax.broadcasted_iota(jnp.int32, own.shape, 1)
    lane = lax.broadcasted_iota(jnp.int32, (chips, LANES), 1)
    out_lane = lax.broadcasted_iota(jnp.int32, (chips, slots), 1)
    out_chip = lax.broadcasted_iota(jnp.int32, (chips, slots), 0)
    ids = jnp.zeros((chips, slots), jnp.float32)
    for turn, facts in enumerate((own, other)):
        low = jnp.full((chips, 1), 1e9, jnp.float32)
        high = jnp.full((chips, 1), -1.0, jnp.float32)
        for game in range(rows // steps):

            def pick(i):
                return jnp.sum(jnp.where(kind == 2 * i + game, facts, 0.0), axis=1)

            number = pick(0) * 4096.0 + pick(1) * 64.0 + pick(2)
            hit = (pick(3) == group_index.astype(jnp.float32)) & (lane < steps)
            coded = (game * steps + lane).astype(jnp.float32) * 262144.0 + number
            low = jnp.minimum(low, jnp.min(jnp.where(hit, coded, 1e9), axis=1, keepdims=True))
            high = jnp.maximum(high, jnp.max(jnp.where(hit, coded, -1.0), axis=1, keepdims=True))
        sender = out_chip * CORES + lax.rem(core + turn, CORES)
        for k, (coded, there) in enumerate(((low, high >= 0), (high, high > low))):
            number = (coded.astype(jnp.int32) & 262143).astype(jnp.float32)
            value = jnp.where(there, number, -1.0)
            ids = ids + jnp.where(out_lane == sender * capacity + k, value, 0.0)
    ids_ref[...] = jnp.sum(ids, axis=0, keepdims=True).astype(jnp.int32)


def attend_kernel(
    lengths_ref,
    mine_ref,
    placed_ref,
    shard0_ref,
    shard1_ref,
    shard2_ref,
    shard3_ref,
    packed_ref,
):
    shards = (shard0_ref, shard1_ref, shard2_ref, shard3_ref)
    count, _, rounds, games, block, _ = shard0_ref.shape
    rows = mine_ref.shape[0]
    steps = rows // games
    heads = mine_ref.shape[1] // HEAD - 2
    n_tp = count * len(shards)
    factor = 1.0 / math.sqrt(HEAD)
    mine = mine_ref[...].astype(jnp.float32)
    spot = lax.broadcasted_iota(jnp.int32, (1, count * rounds * block), 1)
    tp_index = lax.axis_index("tp")
    positions = []
    for shift in range(len(shards)):
        across = lax.rem(lax.rem(tp_index, len(shards)) - shift + len(shards), len(shards))
        down = (tp_index // len(shards) - spot // (rounds * block) + count) % count
        tp = down * len(shards) + across
        positions.append((spot // block % rounds * n_tp + tp) * block + spot % block)
    contract = (((1,), (1,)), ((), ()))
    games_out = []
    for game in range(games):
        band = mine[game * steps : (game + 1) * steps]
        queries = jnp.concatenate(
            [band[:, h * HEAD : (h + 1) * HEAD] for h in range(heads)], axis=0
        ).astype(jnp.bfloat16)
        new_keys = band[:, heads * HEAD : (heads + 1) * HEAD].astype(jnp.bfloat16)
        new_values = band[:, (heads + 1) * HEAD :].astype(jnp.bfloat16)
        new_scores = factor * lax.dot_general(
            queries, new_keys, contract, preferred_element_type=jnp.float32
        )
        later = lax.broadcasted_iota(jnp.int32, new_scores.shape, 1)
        step = lax.broadcasted_iota(jnp.int32, new_scores.shape, 0) % steps
        new_valid = later <= step
        top = jnp.max(jnp.where(new_valid, new_scores, NEG_FILL), axis=1, keepdims=True)
        kept = []
        for shard_ref, position in zip(shards, positions):
            keys = shard_ref[:, 0, :, game].reshape(count * rounds * block, HEAD)
            scores = factor * lax.dot_general(
                queries, keys, contract, preferred_element_type=jnp.float32
            )
            scores = jnp.where(position < lengths_ref[game], scores, NEG_FILL)
            top = jnp.maximum(top, jnp.max(scores, axis=1, keepdims=True))
            kept.append(scores)
        weight = jnp.where(new_valid, jnp.exp(new_scores - top), 0.0).astype(jnp.bfloat16)
        total = jnp.sum(weight.astype(jnp.float32), axis=1, keepdims=True)
        mixed = jnp.dot(weight, new_values, preferred_element_type=jnp.float32)
        for shard_ref, position, scores in zip(shards, positions, kept):
            values = shard_ref[:, 1, :, game].reshape(count * rounds * block, HEAD)
            weight = jnp.where(
                position < lengths_ref[game], jnp.exp(scores - top), 0.0
            ).astype(jnp.bfloat16)
            total = total + jnp.sum(weight.astype(jnp.float32), axis=1, keepdims=True)
            mixed = mixed + jnp.dot(weight, values, preferred_element_type=jnp.float32)
        out = mixed / total
        games_out.append(
            jnp.concatenate([out[h * steps : (h + 1) * steps] for h in range(heads)], axis=1)
        )
    attended = jnp.concatenate(games_out, axis=0).astype(jnp.bfloat16)
    packed_ref[...] = jnp.dot(
        placed_ref[...], attended, preferred_element_type=jnp.float32
    ).astype(jnp.bfloat16)


def per_device(
    hidden,
    query_weight,
    key_value_weight,
    query_codes,
    query_scales,
    key_value_codes,
    key_value_scales,
    key_cache,
    value_cache,
    lengths,
    counts,
    learner,
    token_ids,
):
    games, steps, features = hidden.shape
    rows = games * steps
    n_group = lax.axis_size("group")
    n_tp = lax.axis_size("tp")
    chips = n_group // CORES
    across = n_tp // KV_HEADS
    same_core = [[CORES * u + k for u in range(chips)] for k in range(CORES)]
    swap = [(g, g ^ 1) for g in range(n_group)]
    turn = [
        ((CORES * u + k) * n_tp + t, (CORES * t + k) * n_tp + u)
        for u in range(chips)
        for k in range(CORES)
        for t in range(n_tp)
    ]
    wide = HEADS // n_tp * HEAD
    capacity = max(2, 2 * rows // n_group)
    rounds, _, _, block, _ = key_cache.shape
    pair_rows = key_value_codes.shape[1]
    bf16 = jnp.bfloat16

    def far(x):
        return pltpu.with_memory_space_constraint(x, pltpu.HBM)


    load, named = pl.pallas_call(
        load_kernel,
        out_shape=[
            jax.ShapeDtypeStruct((chips, 2 * TILE, 3 * LANES), bf16),
            jax.ShapeDtypeStruct((1, rows), jnp.int32),
        ],
        in_specs=[HBM] * 6,
        out_specs=[VMEM] * 2,
        scratch_shapes=[
            pltpu.SMEM((games,), jnp.int32),
            pltpu.VMEM((rows, features), bf16),
            pltpu.VMEM((pair_rows, 2 * KV_HEADS * HEAD), bf16),
            pltpu.VMEM((2 * KV_HEADS, pair_rows), jnp.float32),
            pltpu.VMEM((games, 1, steps), jnp.int32),
            pltpu.VMEM((games, steps), jnp.int32),
            pltpu.SemaphoreType.DMA((6,)),
        ],
        compiler_params=PARAMS,
        name="load",
    )(
        far(counts),
        far(hidden.reshape(rows, features)),
        far(key_value_codes[0]),
        far(key_value_scales[0].T),
        far(learner.transpose(0, 2, 1)),
        far(token_ids),
    )
    came = lax.all_to_all(
        load, "group", split_axis=0, concat_axis=0, tiled=True, axis_index_groups=same_core
    )

    piece = jax.ShapeDtypeStruct((2, rounds, games, block, HEAD), bf16)
    query_delta, *pieces = pl.pallas_call(
        pieces_kernel,
        out_shape=[jax.ShapeDtypeStruct(query_codes.shape, bf16)] + [piece] * KV_HEADS,
        in_specs=[HBM] * 4,
        out_specs=[VMEM] * (1 + KV_HEADS),
        scratch_shapes=[
            pltpu.VMEM(query_codes.shape, bf16),
            pltpu.VMEM((1, features), jnp.float32),
            pltpu.SemaphoreType.DMA((2,)),
            pltpu.SemaphoreType.DMA((2 * KV_HEADS,)),
        ],
        compiler_params=PARAMS,
        name="pieces",
    )(far(query_codes), far(query_scales.T), far(key_cache), far(value_cache))
    for shift in range(1, KV_HEADS):
        pairs = [(t, (t + shift * across) % n_tp) for t in range(n_tp)]
        pieces[shift] = lax.ppermute(pieces[shift], "tp", pairs)
    other = pl.pallas_call(
        swap_kernel,
        out_shape=jax.ShapeDtypeStruct((3 * chips * TILE + features, LANES), bf16),
        in_specs=[VMEM] * 2 + [ANY] * (KV_HEADS - 1),
        out_specs=VMEM,
        compiler_params=PARAMS,
        name="swap",
    )(came, query_delta, *pieces[1:])
    other = lax.ppermute(other, "group", swap)

    part = pl.pallas_call(
        part_kernel,
        out_shape=jax.ShapeDtypeStruct((chips, rows, wide + 2 * HEAD), jnp.float32),
        in_specs=[VMEM] * 3 + [HBM] * 2,
        out_specs=VMEM,
        scratch_shapes=[
            pltpu.VMEM((features, wide), bf16),
            pltpu.VMEM((features, HEAD), bf16),
            pltpu.VMEM((features, HEAD), bf16),
            pltpu.SemaphoreType.DMA((3,)),
        ],
        compiler_params=PARAMS,
        name="part",
    )(came, other, query_delta, far(query_weight), far(key_value_weight))
    parts = lax.all_to_all(part, "tp", split_axis=0, concat_axis=0, tiled=True)

    shard = pl.pallas_call(
        join_kernel,
        out_shape=jax.ShapeDtypeStruct((KV_HEADS,) + piece.shape, bf16),
        in_specs=[ANY] + [VMEM] * KV_HEADS,
        out_specs=VMEM,
        compiler_params=PARAMS,
        name="join",
    )(part, *pieces)
    shards = [shard]
    for shift in range(1, across):
        pairs = [(t, t // across * across + (t + shift) % across) for t in range(n_tp)]
        shards.append(lax.ppermute(shard, "tp", pairs))
    mine = jnp.sum(parts, axis=0).astype(bf16)
    mine = lax.ppermute(mine, ("group", "tp"), turn)

    placed, ids_back = pl.pallas_call(
        facts_kernel,
        out_shape=[
            jax.ShapeDtypeStruct((n_group * capacity, rows), bf16),
            jax.ShapeDtypeStruct((1, n_group * capacity), jnp.int32),
        ],
        in_specs=[ANY] + [VMEM] * 3,
        out_specs=[VMEM] * 2,
        compiler_params=PARAMS,
        name="facts",
    )(parts, named, came, other)

    packed = pl.pallas_call(
        attend_kernel,
        out_shape=jax.ShapeDtypeStruct((n_group * capacity, wide), bf16),
        in_specs=[SMEM] + [VMEM] * 6,
        out_specs=VMEM,
        compiler_params=PARAMS,
        name="attend",
    )(lengths, mine, placed, *shards)
    packed = packed.reshape(n_group, capacity, wide)
    rows_back = lax.all_to_all(packed, "group", split_axis=0, concat_axis=1, tiled=True)
    return (rows_back, ids_back)


def solution(mesh):
    placed = (
        P("group", None, "tp"),
        P("tp", None),
        P("tp", None),
        P("tp", "group"),
        P("tp", "group"),
        P("tp", "group", None),
        P("tp", "group", None),
        P(None, "tp", "group", None, None),
        P(None, "tp", "group", None, None),
        P("group"),
        P("group"),
        P("group", None, None),
        P("group", None),
    )
    return jax.shard_map(
        per_device,
        mesh=mesh,
        in_specs=placed,
        out_specs=(P("group", None, "tp"), P("group", None)),
        check_vma=False,
    )
```

```python
import math

import jax
import jax.numpy as jnp
from jax import lax
from jax.experimental import pallas as pl
from jax.experimental.pallas import tpu as pltpu
from jax.sharding import PartitionSpec as P

HEADS = 32
KV_HEADS = 4
HEAD = 128
CORES = 2
SIDES = 2
LANES = 128


NEG_FILL = -1e30

VMEM = pl.BlockSpec(memory_space=pltpu.VMEM)
SMEM = pl.BlockSpec(memory_space=pltpu.SMEM)
HBM = pl.BlockSpec(memory_space=pltpu.HBM)
ANY = pl.BlockSpec(memory_space=pl.ANY)
PARAMS = pltpu.CompilerParams(vmem_limit_bytes=24 * 1024 * 1024)


def column(row):
    n = row.shape[1]
    across = lax.broadcasted_iota(jnp.int32, (n, n), 1)
    down = lax.broadcasted_iota(jnp.int32, (n, n), 0)
    return jnp.sum(jnp.where(across == down, row, jnp.zeros_like(row)), axis=1, keepdims=True)


def fetch(pairs, sems):
    copies = [
        pltpu.make_async_copy(source, target, sems.at[i]) for i, (source, target) in enumerate(pairs)
    ]
    for copy in copies:
        copy.start()
    return copies


def load_kernel(
    counts_hbm,
    hidden_hbm,
    codes_hbm,
    scales_hbm,
    learner_hbm,
    ids_hbm,
    load_ref,
    named_ref,
    counts_ref,
    hidden_ref,
    codes_ref,
    scales_ref,
    learner_ref,
    ids_ref,
    sems,
):
    copies = fetch(
        [
            (codes_hbm, codes_ref),
            (scales_hbm, scales_ref),
            (hidden_hbm, hidden_ref),
            (counts_hbm, counts_ref),
            (learner_hbm, learner_ref),
            (ids_hbm, ids_ref),
        ],
        sems,
    )
    peers = load_ref.shape[0]
    games, steps, features = hidden_ref.shape
    for copy in copies:
        copy.wait()
    inputs = jnp.concatenate(
        [hidden_ref[game].astype(jnp.float32) for game in range(games)], axis=1
    ).astype(jnp.bfloat16)
    load_ref[:, :, : games * features] = jnp.broadcast_to(inputs, (peers,) + inputs.shape)
    step = lax.broadcasted_iota(jnp.int32, (1, steps), 1)
    named = [
        jnp.where(step < counts_ref[game], learner_ref[game], -1) for game in range(games)
    ]
    named = jnp.concatenate(named, axis=1)
    named_ref[...] = named
    ids = jnp.concatenate([ids_ref[game : game + 1] for game in range(games)], axis=1)
    facts = jnp.concatenate([ids >> 12, (ids >> 6) & 63, ids & 63, named], axis=0)
    facts = jnp.concatenate(
        [facts.astype(jnp.float32), jnp.zeros((4, LANES - games * steps), jnp.float32)], axis=1
    )
    extra = codes_ref.shape[0] - steps
    blank = jnp.zeros((steps - 4 - extra, LANES), jnp.float32)
    for block in range(2 * KV_HEADS):
        scale = column(scales_ref[block : block + 1, :])
        delta = codes_ref[:, block * HEAD : (block + 1) * HEAD].astype(jnp.float32) * scale
        rest = jnp.concatenate([delta[steps:], blank, facts], axis=0)
        cell = jnp.concatenate([delta[:steps], rest], axis=1).astype(jnp.bfloat16)
        head, part = block % KV_HEADS, block // KV_HEADS
        for peer in range(part, peers, CORES):
            if peer * KV_HEADS // peers == head:
                load_ref[peer, :, games * features :] = cell


def pieces_kernel(
    codes_hbm,
    scales_hbm,
    key_hbm,
    value_hbm,
    delta_ref,
    piece0_ref,
    piece1_ref,
    piece2_ref,
    piece3_ref,
    codes_ref,
    scales_ref,
    sems,
    piece_sems,
):
    copies = fetch([(codes_hbm, codes_ref), (scales_hbm, scales_ref)], sems)
    own = lax.axis_index("tp") // (lax.axis_size("tp") // KV_HEADS)
    moves = []
    for shift, piece_ref in enumerate((piece0_ref, piece1_ref, piece2_ref, piece3_ref)):
        head = own ^ shift
        lanes = pl.ds(pl.multiple_of(head * HEAD, HEAD), HEAD)
        for part, cache_hbm in enumerate((key_hbm, value_hbm)):
            moves.append((cache_hbm.at[:, 0, :, :, lanes], piece_ref.at[part]))
    moves = fetch(moves, piece_sems)
    for copy in copies:
        copy.wait()
    scale = column(scales_ref[...])
    delta_ref[...] = (codes_ref[...].astype(jnp.float32) * scale).astype(jnp.bfloat16)
    for copy in moves:
        copy.wait()


def cells_of(came_ref, start, size):
    peers, steps, _ = came_ref.shape
    cell = came_ref[:, :, start : start + size].astype(jnp.float32)
    return cell.reshape(peers * steps, size).astype(jnp.bfloat16)


def swap_kernel(came_ref, after1_ref, after2_ref, after3_ref, out_ref):
    _, block, lanes = out_ref.shape
    width = came_ref.shape[2]
    for i in range(2):
        out_ref[i] = cells_of(came_ref, width - (2 - i) * lanes, lanes)


def dot(a, b):
    return jnp.dot(a, b, preferred_element_type=jnp.float32)


def part_kernel(
    came_ref,
    mine_ref,
    other_ref,
    query_hbm,
    pair_hbm,
    queries_ref,
    pairs_ref,
    spread_ref,
    weight_ref,
    sems,
):
    peers, steps, width = came_ref.shape
    features = weight_ref.shape[1]
    rows = queries_ref.shape[1]
    games = rows // steps
    block = peers * steps
    group_index = lax.axis_index("group")
    level = group_index // (SIDES * CORES)
    side, core = lax.rem(group_index // CORES, SIDES), lax.rem(group_index, CORES)
    head = level * KV_HEADS // (peers // CORES)
    pair_rows = features // (peers * SIDES)

    def columns(source, index):
        return source.at[:, pl.ds(pl.multiple_of(index * HEAD, HEAD), HEAD)]

    copies = fetch(
        [
            (columns(query_hbm, (level * SIDES + 0) * CORES + core), weight_ref.at[0]),
            (columns(query_hbm, (level * SIDES + 1) * CORES + core), weight_ref.at[1]),
            (columns(pair_hbm, core * KV_HEADS + head), weight_ref.at[2]),
        ],
        sems,
    )
    inputs = jnp.concatenate(
        [cells_of(came_ref, game * features, features) for game in range(games)], axis=0
    )
    spot = lax.broadcasted_iota(jnp.int32, (1, 2 * block), 1)
    feature = lax.broadcasted_iota(jnp.int32, (features, 2 * block), 0)
    peer, step = spot % block // steps, spot % steps
    offset = jnp.where(spot < block, step, step + steps)
    spreads = []
    for turn in range(SIDES):
        owner = (peer // CORES * SIDES + (side ^ turn)) * CORES + peer % CORES
        source = jnp.where(offset < pair_rows, owner * pair_rows + offset, -1)
        spread = (feature == source).astype(jnp.float32).astype(jnp.bfloat16)
        spreads.append(dot(inputs, spread).astype(jnp.bfloat16))
    spread_ref[...] = spreads[1]
    pairs = dot(spreads[0][:, :block], cells_of(came_ref, width - 2 * LANES, LANES))
    pairs = pairs + dot(spreads[0][:, block:], cells_of(came_ref, width - LANES, LANES))
    mine, other = mine_ref[...], other_ref[...]
    first = dot(inputs, jnp.where(side == 0, mine, other))
    second = dot(inputs, jnp.where(side == 0, other, mine))
    for copy in copies:
        copy.wait()

    def put(ref, i, sums):
        for game in range(games):
            ref[:, game * steps : (game + 1) * steps, i * HEAD : (i + 1) * HEAD] = sums[
                game * block : (game + 1) * block
            ].reshape(peers, steps, HEAD)

    put(queries_ref, 0, first + dot(inputs, weight_ref[0]))
    put(queries_ref, 1, second + dot(inputs, weight_ref[1]))
    put(pairs_ref, 0, pairs + dot(inputs, weight_ref[2]))


def whole_kernel(queries_ref, pairs_ref, spread_ref, other_ref, after_ref, part_ref):
    peers, rows, wide = queries_ref.shape
    block = spread_ref.shape[1] // 2
    games = spread_ref.shape[0] // block
    steps = rows // games
    part_ref[:, :, :wide] = queries_ref[...]
    pairs = dot(spread_ref[:, :block], other_ref[0]) + dot(spread_ref[:, block:], other_ref[1])
    for game in range(games):
        band = slice(game * steps, (game + 1) * steps)
        part_ref[:, band, wide:] = pairs_ref[:, band, :] + pairs[
            game * block : (game + 1) * block
        ].reshape(peers, steps, HEAD)


def sum_kernel(parts_ref, keep_ref, give_ref):
    core = lax.rem(lax.axis_index("group"), CORES)
    sums = jnp.sum(parts_ref[...], axis=0)
    heads = [sums[:, i * HEAD : (i + 1) * HEAD] for i in range(3)]
    keep_ref[:, :HEAD] = jnp.where(core == 0, heads[0], heads[1]).astype(jnp.bfloat16)
    give_ref[:, :HEAD] = jnp.where(core == 0, heads[1], heads[0]).astype(jnp.bfloat16)
    keep_ref[:, HEAD:] = heads[2].astype(jnp.bfloat16)
    give_ref[:, HEAD:] = heads[2].astype(jnp.bfloat16)


def join_kernel(after_ref, *refs):
    shard_ref = refs[-1]
    for shift, piece_ref in enumerate(refs[:-1]):
        shard_ref[shift] = piece_ref[...]


def facts_kernel(after_ref, named_ref, came_ref, other_ref, placed_ref, ids_ref):
    peers, steps, width = came_ref.shape
    slots, rows = placed_ref.shape
    group_index = lax.axis_index("group")
    side = lax.rem(group_index // CORES, SIDES)
    capacity = slots // (peers * SIDES)

    named = named_ref[...].astype(jnp.float32)
    before = lax.broadcasted_iota(jnp.int32, (rows, rows), 0) < lax.broadcasted_iota(
        jnp.int32, (rows, rows), 1
    )
    rank = jnp.sum(jnp.where((column(named) == named) & before, 1.0, 0.0), axis=0, keepdims=True)
    slot = jnp.where(named >= 0, named * capacity + rank, -1.0)
    index = lax.broadcasted_iota(jnp.int32, (slots, rows), 0).astype(jnp.float32)
    placed_ref[...] = jnp.where(index == slot, 1.0, 0.0).astype(jnp.bfloat16)

    own = came_ref[:, :, width - LANES :].astype(jnp.float32)
    other = other_ref[1].astype(jnp.float32).reshape(own.shape)
    kind = lax.broadcasted_iota(jnp.int32, own.shape, 1) - (steps - 4)
    lane = lax.broadcasted_iota(jnp.int32, (peers, LANES), 1)
    out_lane = lax.broadcasted_iota(jnp.int32, (peers, slots), 1)
    out_peer = lax.broadcasted_iota(jnp.int32, (peers, slots), 0)
    ids = jnp.zeros((peers, slots), jnp.float32)
    for turn, facts in enumerate((own, other)):

        def pick(i):
            return jnp.sum(jnp.where(kind == i, facts, 0.0), axis=1)

        number = pick(0) * 4096.0 + pick(1) * 64.0 + pick(2)
        hit = (pick(3) == group_index.astype(jnp.float32)) & (lane < rows)
        coded = lane.astype(jnp.float32) * 262144.0 + number
        low = jnp.min(jnp.where(hit, coded, 1e9), axis=1, keepdims=True)
        high = jnp.max(jnp.where(hit, coded, -1.0), axis=1, keepdims=True)
        sender = (out_peer // CORES * SIDES + (side ^ turn)) * CORES + out_peer % CORES
        for k, (coded, there) in enumerate(((low, high >= 0), (high, high > low))):
            number = (coded.astype(jnp.int32) & 262143).astype(jnp.float32)
            value = jnp.where(there, number, -1.0)
            ids = ids + jnp.where(out_lane == sender * capacity + k, value, 0.0)
    ids_ref[...] = jnp.sum(ids, axis=0, keepdims=True).astype(jnp.int32)


def attend_kernel(
    lengths_ref,
    mine_ref,
    placed_ref,
    shard0_ref,
    shard1_ref,
    shard2_ref,
    shard3_ref,
    packed_ref,
):
    shards = (shard0_ref, shard1_ref, shard2_ref, shard3_ref)
    count, _, rounds, games, block, _ = shard0_ref.shape
    rows = mine_ref.shape[0]
    steps = rows // games
    heads = CORES
    n_tp = count * len(shards)
    factor = 1.0 / math.sqrt(HEAD)
    mine = mine_ref[...].astype(jnp.float32)
    first, second = mine[:, : 2 * HEAD], mine[:, 2 * HEAD :]
    even = lax.rem(lax.axis_index("tp"), 2) == 0
    with_keys, with_values = jnp.where(even, first, second), jnp.where(even, second, first)
    spot = lax.broadcasted_iota(jnp.int32, (1, count * rounds * block), 1)
    tp_index = lax.axis_index("tp")
    positions = []
    for shift in range(len(shards)):
        across = lax.rem(tp_index, len(shards)) ^ shift
        down = (tp_index // len(shards)) ^ (spot // (rounds * block))
        tp = down * len(shards) + across
        positions.append((spot // block % rounds * n_tp + tp) * block + spot % block)
    contract = (((1,), (1,)), ((), ()))
    games_out = []
    for game in range(games):
        bands = [x[game * steps : (game + 1) * steps] for x in (with_keys, with_values)]
        queries = jnp.concatenate([band[:, :HEAD] for band in bands], axis=0).astype(jnp.bfloat16)
        new_keys, new_values = [band[:, HEAD:].astype(jnp.bfloat16) for band in bands]
        new_scores = factor * lax.dot_general(
            queries, new_keys, contract, preferred_element_type=jnp.float32
        )
        later = lax.broadcasted_iota(jnp.int32, new_scores.shape, 1)
        step = lax.broadcasted_iota(jnp.int32, new_scores.shape, 0) % steps
        new_valid = later <= step
        top = jnp.max(jnp.where(new_valid, new_scores, NEG_FILL), axis=1, keepdims=True)
        kept = []
        for shard_ref, position in zip(shards, positions):
            keys = shard_ref[:, 0, :, game].reshape(count * rounds * block, HEAD)
            scores = factor * lax.dot_general(
                queries, keys, contract, preferred_element_type=jnp.float32
            )
            scores = jnp.where(position < lengths_ref[game], scores, NEG_FILL)
            top = jnp.maximum(top, jnp.max(scores, axis=1, keepdims=True))
            kept.append(scores)
        weight = jnp.where(new_valid, jnp.exp(new_scores - top), 0.0).astype(jnp.bfloat16)
        total = jnp.sum(weight.astype(jnp.float32), axis=1, keepdims=True)
        mixed = jnp.dot(weight, new_values, preferred_element_type=jnp.float32)
        for shard_ref, position, scores in zip(shards, positions, kept):
            values = shard_ref[:, 1, :, game].reshape(count * rounds * block, HEAD)
            weight = jnp.where(
                position < lengths_ref[game], jnp.exp(scores - top), 0.0
            ).astype(jnp.bfloat16)
            total = total + jnp.sum(weight.astype(jnp.float32), axis=1, keepdims=True)
            mixed = mixed + jnp.dot(weight, values, preferred_element_type=jnp.float32)
        out = mixed / total
        games_out.append(
            jnp.concatenate([out[h * steps : (h + 1) * steps] for h in range(heads)], axis=1)
        )
    attended = jnp.concatenate(games_out, axis=0).astype(jnp.bfloat16)
    packed_ref[...] = jnp.dot(
        placed_ref[...], attended, preferred_element_type=jnp.float32
    ).astype(jnp.bfloat16)


def per_device(
    hidden,
    query_weight,
    key_value_weight,
    query_codes,
    query_scales,
    key_value_codes,
    key_value_scales,
    key_cache,
    value_cache,
    lengths,
    counts,
    learner,
    token_ids,
):
    games, steps, features = hidden.shape
    rows = games * steps
    n_group = lax.axis_size("group")
    n_tp = lax.axis_size("tp")
    peers = n_group // SIDES
    across = n_tp // KV_HEADS
    near = [
        [g for g in range(n_group) if g // CORES % SIDES == side] for side in range(SIDES)
    ]
    turn = []
    for g in range(n_group):
        level, side, core = g // (SIDES * CORES), g // CORES % SIDES, g % CORES
        for t in range(n_tp):
            to = (t // CORES * SIDES + side) * CORES + t % CORES
            turn.append((g * n_tp + t, to * n_tp + level * CORES + core))
    wide = HEADS // n_tp * HEAD
    capacity = max(2, 2 * rows // n_group)
    rounds, _, _, block, _ = key_cache.shape
    pair_rows = key_value_codes.shape[1]
    bf16 = jnp.bfloat16

    def far(x):
        return pltpu.with_memory_space_constraint(x, pltpu.HBM)


    def along(x, axis, shift):
        return lax.ppermute(x, axis, [(i, i ^ shift) for i in range(lax.axis_size(axis))])

    load, named = pl.pallas_call(
        load_kernel,
        out_shape=[
            jax.ShapeDtypeStruct((peers, steps, games * features + 2 * LANES), bf16),
            jax.ShapeDtypeStruct((1, rows), jnp.int32),
        ],
        in_specs=[HBM] * 6,
        out_specs=[VMEM] * 2,
        scratch_shapes=[
            pltpu.SMEM((games,), jnp.int32),
            pltpu.VMEM(hidden.shape, bf16),
            pltpu.VMEM((pair_rows, 2 * KV_HEADS * HEAD), bf16),
            pltpu.VMEM((2 * KV_HEADS, pair_rows), jnp.float32),
            pltpu.VMEM((games, 1, steps), jnp.int32),
            pltpu.VMEM((games, steps), jnp.int32),
            pltpu.SemaphoreType.DMA((6,)),
        ],
        compiler_params=PARAMS,
        name="load",
    )(
        far(counts),
        far(hidden),
        far(key_value_codes[0]),
        far(key_value_scales[0].T),
        far(learner.transpose(0, 2, 1)),
        far(token_ids),
    )
    came = lax.all_to_all(
        load, "group", split_axis=0, concat_axis=0, tiled=True, axis_index_groups=near
    )

    piece = jax.ShapeDtypeStruct((2, rounds, games, block, HEAD), bf16)
    query_delta, *pieces = pl.pallas_call(
        pieces_kernel,
        out_shape=[jax.ShapeDtypeStruct(query_codes.shape, bf16)] + [piece] * KV_HEADS,
        in_specs=[HBM] * 4,
        out_specs=[VMEM] * (1 + KV_HEADS),
        scratch_shapes=[
            pltpu.VMEM(query_codes.shape, bf16),
            pltpu.VMEM((1, features), jnp.float32),
            pltpu.SemaphoreType.DMA((2,)),
            pltpu.SemaphoreType.DMA((2 * KV_HEADS,)),
        ],
        compiler_params=PARAMS,
        name="pieces",
    )(far(query_codes), far(query_scales.T), far(key_cache), far(value_cache))
    for shift in range(1, KV_HEADS):
        pieces[shift] = along(pieces[shift], "tp", shift * across)
    query_other = along(query_delta, "group", CORES)
    rows_all = peers * steps
    other = pl.pallas_call(
        swap_kernel,
        out_shape=jax.ShapeDtypeStruct((2, rows_all, LANES), bf16),
        in_specs=[VMEM] + [ANY] * (KV_HEADS - 1),
        out_specs=VMEM,
        compiler_params=PARAMS,
        name="swap",
    )(came, *pieces[1:])
    other = along(other, "group", CORES)

    queries, pairs, spread = pl.pallas_call(
        part_kernel,
        out_shape=[
            jax.ShapeDtypeStruct((peers, rows, wide), jnp.float32),
            jax.ShapeDtypeStruct((peers, rows, HEAD), jnp.float32),
            jax.ShapeDtypeStruct((games * rows_all, 2 * rows_all), bf16),
        ],
        in_specs=[VMEM] * 3 + [HBM] * 2,
        out_specs=[VMEM] * 3,
        scratch_shapes=[
            pltpu.VMEM((3, features, HEAD), bf16),
            pltpu.SemaphoreType.DMA((3,)),
        ],
        compiler_params=PARAMS,
        name="part",
    )(came, query_delta, query_other, far(query_weight), far(key_value_weight))
    part = pl.pallas_call(
        whole_kernel,
        out_shape=jax.ShapeDtypeStruct((peers, rows, wide + HEAD), jnp.float32),
        in_specs=[VMEM] * 4 + [ANY],
        out_specs=VMEM,
        compiler_params=PARAMS,
        name="whole",
    )(queries, pairs, spread, other, pieces[1])
    parts = lax.all_to_all(part, "tp", split_axis=0, concat_axis=0, tiled=True)

    shard = pl.pallas_call(
        join_kernel,
        out_shape=jax.ShapeDtypeStruct((KV_HEADS,) + piece.shape, bf16),
        in_specs=[ANY] + [VMEM] * KV_HEADS,
        out_specs=VMEM,
        compiler_params=PARAMS,
        name="join",
    )(part, *pieces)
    shards = [shard]
    for shift in range(1, across):
        shards.append(along(shard, "tp", shift))
    keep, give = pl.pallas_call(
        sum_kernel,
        out_shape=[jax.ShapeDtypeStruct((rows, 2 * HEAD), bf16)] * 2,
        in_specs=[VMEM],
        out_specs=[VMEM] * 2,
        compiler_params=PARAMS,
        name="sum",
    )(parts)
    got = along(give, "group", 1)
    mine = lax.ppermute(jnp.concatenate([keep, got], axis=1), ("group", "tp"), turn)

    placed, ids_back = pl.pallas_call(
        facts_kernel,
        out_shape=[
            jax.ShapeDtypeStruct((n_group * capacity, rows), bf16),
            jax.ShapeDtypeStruct((1, n_group * capacity), jnp.int32),
        ],
        in_specs=[ANY] + [VMEM] * 3,
        out_specs=[VMEM] * 2,
        compiler_params=PARAMS,
        name="facts",
    )(parts, named, came, other)

    packed = pl.pallas_call(
        attend_kernel,
        out_shape=jax.ShapeDtypeStruct((n_group * capacity, wide), bf16),
        in_specs=[SMEM] + [VMEM] * 6,
        out_specs=VMEM,
        compiler_params=PARAMS,
        name="attend",
    )(lengths, mine, placed, *shards)
    packed = packed.reshape(n_group, capacity, wide)
    rows_back = lax.all_to_all(packed, "group", split_axis=0, concat_axis=1, tiled=True)
    return (rows_back, ids_back)


def solution(mesh):
    placed = (
        P("group", None, "tp"),
        P("tp", None),
        P("tp", None),
        P("tp", "group"),
        P("tp", "group"),
        P("tp", "group", None),
        P("tp", "group", None),
        P(None, "tp", "group", None, None),
        P(None, "tp", "group", None, None),
        P("group"),
        P("group"),
        P("group", None, None),
        P("group", None),
    )
    return jax.shard_map(
        per_device,
        mesh=mesh,
        in_specs=placed,
        out_specs=(P("group", None, "tp"), P("group", None)),
        check_vma=False,
    )
```

```python
import math

import jax
import jax.numpy as jnp
from jax import lax
from jax.experimental import pallas as pl
from jax.experimental.pallas import tpu as pltpu
from jax.sharding import PartitionSpec as P

HEADS = 32
KV_HEADS = 4
HEAD = 128
CORES = 2
SIDES = 2
LANES = 128


NEG_FILL = -1e30

VMEM = pl.BlockSpec(memory_space=pltpu.VMEM)
SMEM = pl.BlockSpec(memory_space=pltpu.SMEM)
HBM = pl.BlockSpec(memory_space=pltpu.HBM)
ANY = pl.BlockSpec(memory_space=pl.ANY)
PARAMS = pltpu.CompilerParams(vmem_limit_bytes=24 * 1024 * 1024)


def column(row):
    n = row.shape[1]
    across = lax.broadcasted_iota(jnp.int32, (n, n), 1)
    down = lax.broadcasted_iota(jnp.int32, (n, n), 0)
    return jnp.sum(jnp.where(across == down, row, jnp.zeros_like(row)), axis=1, keepdims=True)


def fetch(pairs, sems):
    copies = [
        pltpu.make_async_copy(source, target, sems.at[i]) for i, (source, target) in enumerate(pairs)
    ]
    for copy in copies:
        copy.start()
    return copies


def load_kernel(
    counts_hbm,
    hidden_hbm,
    codes_hbm,
    scales_hbm,
    learner_hbm,
    ids_hbm,
    load_ref,
    named_ref,
    counts_ref,
    hidden_ref,
    codes_ref,
    scales_ref,
    learner_ref,
    ids_ref,
    sems,
):
    copies = fetch(
        [
            (codes_hbm, codes_ref),
            (scales_hbm, scales_ref),
            (hidden_hbm, hidden_ref),
            (counts_hbm, counts_ref),
            (learner_hbm, learner_ref),
            (ids_hbm, ids_ref),
        ],
        sems,
    )
    peers = load_ref.shape[0]
    games, steps, features = hidden_ref.shape
    for copy in copies:
        copy.wait()
    inputs = jnp.concatenate(
        [hidden_ref[game].astype(jnp.float32) for game in range(games)], axis=1
    ).astype(jnp.bfloat16)
    load_ref[:, :, : games * features] = jnp.broadcast_to(inputs, (peers,) + inputs.shape)
    step = lax.broadcasted_iota(jnp.int32, (1, steps), 1)
    named = [
        jnp.where(step < counts_ref[game], learner_ref[game], -1) for game in range(games)
    ]
    named = jnp.concatenate(named, axis=1)
    named_ref[...] = named
    ids = jnp.concatenate([ids_ref[game : game + 1] for game in range(games)], axis=1)
    facts = jnp.concatenate([ids >> 12, (ids >> 6) & 63, ids & 63, named], axis=0)
    facts = jnp.concatenate(
        [facts.astype(jnp.float32), jnp.zeros((4, LANES - games * steps), jnp.float32)], axis=1
    )
    extra = codes_ref.shape[0] - steps
    blank = jnp.zeros((steps - 4 - extra, LANES), jnp.float32)
    for block in range(2 * KV_HEADS):
        scale = column(scales_ref[block : block + 1, :])
        delta = codes_ref[:, block * HEAD : (block + 1) * HEAD].astype(jnp.float32) * scale
        rest = jnp.concatenate([delta[steps:], blank, facts], axis=0)
        cell = jnp.concatenate([delta[:steps], rest], axis=1).astype(jnp.bfloat16)
        head, part = block % KV_HEADS, block // KV_HEADS
        for peer in range(part, peers, CORES):
            if peer * KV_HEADS // peers == head:
                load_ref[peer, :, games * features :] = cell


def pieces_kernel(
    codes_hbm,
    scales_hbm,
    key_hbm,
    value_hbm,
    delta_ref,
    piece0_ref,
    piece1_ref,
    piece2_ref,
    piece3_ref,
    codes_ref,
    scales_ref,
    sems,
    piece_sems,
):
    copies = fetch([(codes_hbm, codes_ref), (scales_hbm, scales_ref)], sems)
    own = lax.axis_index("tp") // (lax.axis_size("tp") // KV_HEADS)
    moves = []
    for shift, piece_ref in enumerate((piece0_ref, piece1_ref, piece2_ref, piece3_ref)):
        head = own ^ shift
        lanes = pl.ds(pl.multiple_of(head * HEAD, HEAD), HEAD)
        for part, cache_hbm in enumerate((key_hbm, value_hbm)):
            moves.append((cache_hbm.at[:, 0, :, :, lanes], piece_ref.at[part]))
    moves = fetch(moves, piece_sems)
    for copy in copies:
        copy.wait()
    scale = column(scales_ref[...])
    delta_ref[...] = (codes_ref[...].astype(jnp.float32) * scale).astype(jnp.bfloat16)
    for copy in moves:
        copy.wait()


def cells_of(came_ref, start, size):
    peers, steps, _ = came_ref.shape
    cell = came_ref[:, :, start : start + size].astype(jnp.float32)
    return cell.reshape(peers * steps, size).astype(jnp.bfloat16)


def swap_kernel(came_ref, out_ref):
    _, block, lanes = out_ref.shape
    width = came_ref.shape[2]
    for i in range(2):
        out_ref[i] = cells_of(came_ref, width - (2 - i) * lanes, lanes)


def dot(a, b):
    return jnp.dot(a, b, preferred_element_type=jnp.float32)


def part_kernel(
    came_ref,
    mine_ref,
    other_ref,
    query_hbm,
    pair_hbm,
    queries_ref,
    pairs_ref,
    spread_ref,
    weight_ref,
    sems,
):
    peers, steps, width = came_ref.shape
    features = weight_ref.shape[1]
    rows = queries_ref.shape[1]
    games = rows // steps
    block = peers * steps
    group_index = lax.axis_index("group")
    level = group_index // (SIDES * CORES)
    side, core = lax.rem(group_index // CORES, SIDES), lax.rem(group_index, CORES)
    head = level * KV_HEADS // (peers // CORES)
    pair_rows = features // (peers * SIDES)

    def columns(source, index):
        return source.at[:, pl.ds(pl.multiple_of(index * HEAD, HEAD), HEAD)]

    copies = fetch(
        [
            (columns(query_hbm, (level * SIDES + 0) * CORES + core), weight_ref.at[0]),
            (columns(query_hbm, (level * SIDES + 1) * CORES + core), weight_ref.at[1]),
            (columns(pair_hbm, core * KV_HEADS + head), weight_ref.at[2]),
        ],
        sems,
    )
    inputs = jnp.concatenate(
        [cells_of(came_ref, game * features, features) for game in range(games)], axis=0
    )
    spot = lax.broadcasted_iota(jnp.int32, (1, 2 * block), 1)
    feature = lax.broadcasted_iota(jnp.int32, (features, 2 * block), 0)
    peer, step = spot % block // steps, spot % steps
    offset = jnp.where(spot < block, step, step + steps)
    spreads = []
    for turn in range(SIDES):
        owner = (peer // CORES * SIDES + (side ^ turn)) * CORES + peer % CORES
        source = jnp.where(offset < pair_rows, owner * pair_rows + offset, -1)
        spread = (feature == source).astype(jnp.float32).astype(jnp.bfloat16)
        spreads.append(dot(inputs, spread).astype(jnp.bfloat16))
    spread_ref[...] = spreads[1]
    pairs = dot(spreads[0][:, :block], cells_of(came_ref, width - 2 * LANES, LANES))
    pairs = pairs + dot(spreads[0][:, block:], cells_of(came_ref, width - LANES, LANES))
    mine, other = mine_ref[...], other_ref[...]
    first = dot(inputs, jnp.where(side == 0, mine, other))
    second = dot(inputs, jnp.where(side == 0, other, mine))
    for copy in copies:
        copy.wait()

    def put(ref, i, sums):
        for game in range(games):
            ref[:, game * steps : (game + 1) * steps, i * HEAD : (i + 1) * HEAD] = sums[
                game * block : (game + 1) * block
            ].reshape(peers, steps, HEAD)

    put(queries_ref, 0, first + dot(inputs, weight_ref[0]))
    put(queries_ref, 1, second + dot(inputs, weight_ref[1]))
    put(pairs_ref, 0, pairs + dot(inputs, weight_ref[2]))


def whole_kernel(queries_ref, pairs_ref, spread_ref, other_ref, after1_ref, after2_ref, after3_ref, part_ref):
    peers, rows, wide = queries_ref.shape
    block = spread_ref.shape[1] // 2
    games = spread_ref.shape[0] // block
    steps = rows // games
    part_ref[:, :, :wide] = queries_ref[...]
    pairs = dot(spread_ref[:, :block], other_ref[0]) + dot(spread_ref[:, block:], other_ref[1])
    for game in range(games):
        band = slice(game * steps, (game + 1) * steps)
        part_ref[:, band, wide:] = pairs_ref[:, band, :] + pairs[
            game * block : (game + 1) * block
        ].reshape(peers, steps, HEAD)


def sum_kernel(parts_ref, keep_ref, give_ref):
    core = lax.rem(lax.axis_index("group"), CORES)
    sums = jnp.sum(parts_ref[...], axis=0)
    heads = [sums[:, i * HEAD : (i + 1) * HEAD] for i in range(3)]
    keep_ref[:, :HEAD] = jnp.where(core == 0, heads[0], heads[1]).astype(jnp.bfloat16)
    give_ref[:, :HEAD] = jnp.where(core == 0, heads[1], heads[0]).astype(jnp.bfloat16)
    keep_ref[:, HEAD:] = heads[2].astype(jnp.bfloat16)
    give_ref[:, HEAD:] = heads[2].astype(jnp.bfloat16)


def join_kernel(after_ref, *refs):
    shard_ref = refs[-1]
    for shift, piece_ref in enumerate(refs[:-1]):
        shard_ref[shift] = piece_ref[...]


def facts_kernel(after_ref, named_ref, came_ref, other_ref, placed_ref, ids_ref):
    peers, steps, width = came_ref.shape
    slots, rows = placed_ref.shape
    group_index = lax.axis_index("group")
    side = lax.rem(group_index // CORES, SIDES)
    capacity = slots // (peers * SIDES)

    named = named_ref[...].astype(jnp.float32)
    before = lax.broadcasted_iota(jnp.int32, (rows, rows), 0) < lax.broadcasted_iota(
        jnp.int32, (rows, rows), 1
    )
    rank = jnp.sum(jnp.where((column(named) == named) & before, 1.0, 0.0), axis=0, keepdims=True)
    slot = jnp.where(named >= 0, named * capacity + rank, -1.0)
    index = lax.broadcasted_iota(jnp.int32, (slots, rows), 0).astype(jnp.float32)
    placed_ref[...] = jnp.where(index == slot, 1.0, 0.0).astype(jnp.bfloat16)

    own = came_ref[:, :, width - LANES :].astype(jnp.float32)
    other = other_ref[1].astype(jnp.float32).reshape(own.shape)
    kind = lax.broadcasted_iota(jnp.int32, own.shape, 1) - (steps - 4)
    lane = lax.broadcasted_iota(jnp.int32, (peers, LANES), 1)
    out_lane = lax.broadcasted_iota(jnp.int32, (peers, slots), 1)
    out_peer = lax.broadcasted_iota(jnp.int32, (peers, slots), 0)
    ids = jnp.zeros((peers, slots), jnp.float32)
    for turn, facts in enumerate((own, other)):

        def pick(i):
            return jnp.sum(jnp.where(kind == i, facts, 0.0), axis=1)

        number = pick(0) * 4096.0 + pick(1) * 64.0 + pick(2)
        hit = (pick(3) == group_index.astype(jnp.float32)) & (lane < rows)
        coded = lane.astype(jnp.float32) * 262144.0 + number
        low = jnp.min(jnp.where(hit, coded, 1e9), axis=1, keepdims=True)
        high = jnp.max(jnp.where(hit, coded, -1.0), axis=1, keepdims=True)
        sender = (out_peer // CORES * SIDES + (side ^ turn)) * CORES + out_peer % CORES
        for k, (coded, there) in enumerate(((low, high >= 0), (high, high > low))):
            number = (coded.astype(jnp.int32) & 262143).astype(jnp.float32)
            value = jnp.where(there, number, -1.0)
            ids = ids + jnp.where(out_lane == sender * capacity + k, value, 0.0)
    ids_ref[...] = jnp.sum(ids, axis=0, keepdims=True).astype(jnp.int32)


def attend_kernel(
    lengths_ref,
    mine_ref,
    placed_ref,
    shard0_ref,
    shard1_ref,
    shard2_ref,
    shard3_ref,
    packed_ref,
):
    shards = (shard0_ref, shard1_ref, shard2_ref, shard3_ref)
    count, _, rounds, games, block, _ = shard0_ref.shape
    rows = mine_ref.shape[0]
    steps = rows // games
    heads = CORES
    n_tp = count * len(shards)
    factor = 1.0 / math.sqrt(HEAD)
    mine = mine_ref[...].astype(jnp.float32)
    first, second = mine[:, : 2 * HEAD], mine[:, 2 * HEAD :]
    even = lax.rem(lax.axis_index("tp"), 2) == 0
    with_keys, with_values = jnp.where(even, first, second), jnp.where(even, second, first)
    spot = lax.broadcasted_iota(jnp.int32, (1, count * rounds * block), 1)
    tp_index = lax.axis_index("tp")
    positions = []
    for shift in range(len(shards)):
        across = lax.rem(tp_index, len(shards)) ^ shift
        down = (tp_index // len(shards)) ^ (spot // (rounds * block))
        tp = down * len(shards) + across
        positions.append((spot // block % rounds * n_tp + tp) * block + spot % block)
    contract = (((1,), (1,)), ((), ()))
    games_out = []
    for game in range(games):
        bands = [x[game * steps : (game + 1) * steps] for x in (with_keys, with_values)]
        queries = jnp.concatenate([band[:, :HEAD] for band in bands], axis=0).astype(jnp.bfloat16)
        new_keys, new_values = [band[:, HEAD:].astype(jnp.bfloat16) for band in bands]
        new_scores = factor * lax.dot_general(
            queries, new_keys, contract, preferred_element_type=jnp.float32
        )
        later = lax.broadcasted_iota(jnp.int32, new_scores.shape, 1)
        step = lax.broadcasted_iota(jnp.int32, new_scores.shape, 0) % steps
        new_valid = later <= step
        top = jnp.max(jnp.where(new_valid, new_scores, NEG_FILL), axis=1, keepdims=True)
        kept = []
        for shard_ref, position in zip(shards, positions):
            keys = shard_ref[:, 0, :, game].reshape(count * rounds * block, HEAD)
            scores = factor * lax.dot_general(
                queries, keys, contract, preferred_element_type=jnp.float32
            )
            scores = jnp.where(position < lengths_ref[game], scores, NEG_FILL)
            top = jnp.maximum(top, jnp.max(scores, axis=1, keepdims=True))
            kept.append(scores)
        weight = jnp.where(new_valid, jnp.exp(new_scores - top), 0.0).astype(jnp.bfloat16)
        total = jnp.sum(weight.astype(jnp.float32), axis=1, keepdims=True)
        mixed = jnp.dot(weight, new_values, preferred_element_type=jnp.float32)
        for shard_ref, position, scores in zip(shards, positions, kept):
            values = shard_ref[:, 1, :, game].reshape(count * rounds * block, HEAD)
            weight = jnp.where(
                position < lengths_ref[game], jnp.exp(scores - top), 0.0
            ).astype(jnp.bfloat16)
            total = total + jnp.sum(weight.astype(jnp.float32), axis=1, keepdims=True)
            mixed = mixed + jnp.dot(weight, values, preferred_element_type=jnp.float32)
        out = mixed / total
        games_out.append(
            jnp.concatenate([out[h * steps : (h + 1) * steps] for h in range(heads)], axis=1)
        )
    attended = jnp.concatenate(games_out, axis=0).astype(jnp.bfloat16)
    packed = jnp.dot(placed_ref[...], attended, preferred_element_type=jnp.float32)
    packed_ref[...] = packed.reshape(packed_ref.shape).astype(jnp.bfloat16)


def per_device(
    hidden,
    query_weight,
    key_value_weight,
    query_codes,
    query_scales,
    key_value_codes,
    key_value_scales,
    key_cache,
    value_cache,
    lengths,
    counts,
    learner,
    token_ids,
):
    games, steps, features = hidden.shape
    rows = games * steps
    n_group = lax.axis_size("group")
    n_tp = lax.axis_size("tp")
    peers = n_group // SIDES
    across = n_tp // KV_HEADS
    near = [
        [g for g in range(n_group) if g // CORES % SIDES == side] for side in range(SIDES)
    ]
    turn = []
    for g in range(n_group):
        level, side, core = g // (SIDES * CORES), g // CORES % SIDES, g % CORES
        for t in range(n_tp):
            to = (t // CORES * SIDES + side) * CORES + t % CORES
            turn.append((g * n_tp + t, to * n_tp + level * CORES + core))
    wide = HEADS // n_tp * HEAD
    capacity = max(2, 2 * rows // n_group)
    rounds, _, _, block, _ = key_cache.shape
    pair_rows = key_value_codes.shape[1]
    bf16 = jnp.bfloat16

    def far(x):
        return pltpu.with_memory_space_constraint(x, pltpu.HBM)


    def along(x, axis, shift):
        return lax.ppermute(x, axis, [(i, i ^ shift) for i in range(lax.axis_size(axis))])

    load, named = pl.pallas_call(
        load_kernel,
        out_shape=[
            jax.ShapeDtypeStruct((peers, steps, games * features + 2 * LANES), bf16),
            jax.ShapeDtypeStruct((1, rows), jnp.int32),
        ],
        in_specs=[HBM] * 6,
        out_specs=[VMEM] * 2,
        scratch_shapes=[
            pltpu.SMEM((games,), jnp.int32),
            pltpu.VMEM(hidden.shape, bf16),
            pltpu.VMEM((pair_rows, 2 * KV_HEADS * HEAD), bf16),
            pltpu.VMEM((2 * KV_HEADS, pair_rows), jnp.float32),
            pltpu.VMEM((games, 1, steps), jnp.int32),
            pltpu.VMEM((games, steps), jnp.int32),
            pltpu.SemaphoreType.DMA((6,)),
        ],
        compiler_params=PARAMS,
        name="load",
    )(
        far(counts),
        far(hidden),
        far(key_value_codes[0]),
        far(key_value_scales[0].T),
        far(learner.transpose(0, 2, 1)),
        far(token_ids),
    )
    came = lax.all_to_all(
        load, "group", split_axis=0, concat_axis=0, tiled=True, axis_index_groups=near
    )

    piece = jax.ShapeDtypeStruct((2, rounds, games, block, HEAD), bf16)
    query_delta, *pieces = pl.pallas_call(
        pieces_kernel,
        out_shape=[jax.ShapeDtypeStruct(query_codes.shape, bf16)] + [piece] * KV_HEADS,
        in_specs=[HBM] * 4,
        out_specs=[VMEM] * (1 + KV_HEADS),
        scratch_shapes=[
            pltpu.VMEM(query_codes.shape, bf16),
            pltpu.VMEM((1, features), jnp.float32),
            pltpu.SemaphoreType.DMA((2,)),
            pltpu.SemaphoreType.DMA((2 * KV_HEADS,)),
        ],
        compiler_params=PARAMS,
        name="pieces",
    )(far(query_codes), far(query_scales.T), far(key_cache), far(value_cache))
    for shift in range(1, KV_HEADS):
        pieces[shift] = along(pieces[shift], "tp", shift * across)
    query_other = along(query_delta, "group", CORES)
    rows_all = peers * steps
    other = pl.pallas_call(
        swap_kernel,
        out_shape=jax.ShapeDtypeStruct((2, rows_all, LANES), bf16),
        in_specs=[VMEM],
        out_specs=VMEM,
        compiler_params=PARAMS,
        name="swap",
    )(came)
    other = along(other, "group", CORES)

    queries, pairs, spread = pl.pallas_call(
        part_kernel,
        out_shape=[
            jax.ShapeDtypeStruct((peers, rows, wide), jnp.float32),
            jax.ShapeDtypeStruct((peers, rows, HEAD), jnp.float32),
            jax.ShapeDtypeStruct((games * rows_all, 2 * rows_all), bf16),
        ],
        in_specs=[VMEM] * 3 + [HBM] * 2,
        out_specs=[VMEM] * 3,
        scratch_shapes=[
            pltpu.VMEM((3, features, HEAD), bf16),
            pltpu.SemaphoreType.DMA((3,)),
        ],
        compiler_params=PARAMS,
        name="part",
    )(came, query_delta, query_other, far(query_weight), far(key_value_weight))
    part = pl.pallas_call(
        whole_kernel,
        out_shape=jax.ShapeDtypeStruct((peers, rows, wide + HEAD), jnp.float32),
        in_specs=[VMEM] * 4 + [ANY] * 3,
        out_specs=VMEM,
        compiler_params=PARAMS,
        name="whole",
    )(queries, pairs, spread, other, *pieces[1:])
    parts = lax.all_to_all(part, "tp", split_axis=0, concat_axis=0, tiled=True)

    shard = pl.pallas_call(
        join_kernel,
        out_shape=jax.ShapeDtypeStruct((KV_HEADS,) + piece.shape, bf16),
        in_specs=[ANY] + [VMEM] * KV_HEADS,
        out_specs=VMEM,
        compiler_params=PARAMS,
        name="join",
    )(part, *pieces)
    shards = [shard]
    for shift in range(1, across):
        shards.append(along(shard, "tp", shift))
    keep, give = pl.pallas_call(
        sum_kernel,
        out_shape=[jax.ShapeDtypeStruct((rows, 2 * HEAD), bf16)] * 2,
        in_specs=[VMEM],
        out_specs=[VMEM] * 2,
        compiler_params=PARAMS,
        name="sum",
    )(parts)
    got = along(give, "group", 1)
    mine = lax.ppermute(jnp.concatenate([keep, got], axis=1), ("group", "tp"), turn)

    placed, ids_back = pl.pallas_call(
        facts_kernel,
        out_shape=[
            jax.ShapeDtypeStruct((n_group * capacity, rows), bf16),
            jax.ShapeDtypeStruct((1, n_group * capacity), jnp.int32),
        ],
        in_specs=[ANY] + [VMEM] * 3,
        out_specs=[VMEM] * 2,
        compiler_params=PARAMS,
        name="facts",
    )(parts, named, came, other)

    packed = pl.pallas_call(
        attend_kernel,
        out_shape=jax.ShapeDtypeStruct((n_group, capacity, wide), bf16),
        in_specs=[SMEM] + [VMEM] * 6,
        out_specs=VMEM,
        compiler_params=PARAMS,
        name="attend",
    )(lengths, mine, placed, *shards)
    rows_back = lax.all_to_all(packed, "group", split_axis=0, concat_axis=1, tiled=True)
    return (rows_back, ids_back)


def solution(mesh):
    placed = (
        P("group", None, "tp"),
        P("tp", None),
        P("tp", None),
        P("tp", "group"),
        P("tp", "group"),
        P("tp", "group", None),
        P("tp", "group", None),
        P(None, "tp", "group", None, None),
        P(None, "tp", "group", None, None),
        P("group"),
        P("group"),
        P("group", None, None),
        P("group", None),
    )
    return jax.shard_map(
        per_device,
        mesh=mesh,
        in_specs=placed,
        out_specs=(P("group", None, "tp"), P("group", None)),
        check_vma=False,
    )
```

```python
import math

import jax
import jax.numpy as jnp
from jax import lax
from jax.experimental import pallas as pl
from jax.experimental.pallas import tpu as pltpu
from jax.sharding import PartitionSpec as P

HEADS = 32
KV_HEADS = 4
HEAD = 128
CORES = 2
SIDES = 2
LANES = 128


NEG_FILL = -1e30

VMEM = pl.BlockSpec(memory_space=pltpu.VMEM)
SMEM = pl.BlockSpec(memory_space=pltpu.SMEM)
HBM = pl.BlockSpec(memory_space=pltpu.HBM)
ANY = pl.BlockSpec(memory_space=pl.ANY)
PARAMS = pltpu.CompilerParams(vmem_limit_bytes=24 * 1024 * 1024)


def whole(shape):
    return pl.BlockSpec(shape, lambda i: (0,) * len(shape))


def column(row):
    n = row.shape[1]
    across = lax.broadcasted_iota(jnp.int32, (n, n), 1)
    down = lax.broadcasted_iota(jnp.int32, (n, n), 0)
    return jnp.sum(jnp.where(across == down, row, jnp.zeros_like(row)), axis=1, keepdims=True)


def fetch(pairs, sems):
    copies = [
        pltpu.make_async_copy(source, target, sems.at[i]) for i, (source, target) in enumerate(pairs)
    ]
    for copy in copies:
        copy.start()
    return copies


def load_kernel(
    counts_ref, hidden_ref, codes_ref, scales_ref, learner_ref, ids_ref, load_ref, named_ref
):
    peers = load_ref.shape[0]
    games, steps, features = hidden_ref.shape
    inputs = jnp.concatenate(
        [hidden_ref[game].astype(jnp.float32) for game in range(games)], axis=1
    ).astype(jnp.bfloat16)
    load_ref[:, :, : games * features] = jnp.broadcast_to(inputs, (peers,) + inputs.shape)
    step = lax.broadcasted_iota(jnp.int32, (1, steps), 1)
    named = [
        jnp.where(step < counts_ref[:, game : game + 1], learner_ref[game], -1)
        for game in range(games)
    ]
    named = jnp.concatenate(named, axis=1)
    named_ref[...] = named
    ids = jnp.concatenate([ids_ref[game : game + 1] for game in range(games)], axis=1)
    facts = jnp.concatenate([ids >> 12, (ids >> 6) & 63, ids & 63, named], axis=0)
    facts = jnp.concatenate(
        [facts.astype(jnp.float32), jnp.zeros((4, LANES - games * steps), jnp.float32)], axis=1
    )
    extra = codes_ref.shape[0] - steps
    blank = jnp.zeros((steps - 4 - extra, LANES), jnp.float32)
    for block in range(2 * KV_HEADS):
        scale = column(scales_ref[block : block + 1, :])
        delta = codes_ref[:, block * HEAD : (block + 1) * HEAD].astype(jnp.float32) * scale
        rest = jnp.concatenate([delta[steps:], blank, facts], axis=0)
        cell = jnp.concatenate([delta[:steps], rest], axis=1).astype(jnp.bfloat16)
        head, part = block % KV_HEADS, block // KV_HEADS
        for peer in range(part, peers, CORES):
            if peer * KV_HEADS // peers == head:
                load_ref[peer, :, games * features :] = cell


def pieces_kernel(
    codes_hbm,
    scales_hbm,
    key_hbm,
    value_hbm,
    delta_ref,
    piece0_ref,
    piece1_ref,
    piece2_ref,
    piece3_ref,
    codes_ref,
    scales_ref,
    sems,
    piece_sems,
):
    copies = fetch([(codes_hbm, codes_ref), (scales_hbm, scales_ref)], sems)
    own = lax.axis_index("tp") // (lax.axis_size("tp") // KV_HEADS)
    moves = []
    for shift, piece_ref in enumerate((piece0_ref, piece1_ref, piece2_ref, piece3_ref)):
        head = own ^ shift
        lanes = pl.ds(pl.multiple_of(head * HEAD, HEAD), HEAD)
        for part, cache_hbm in enumerate((key_hbm, value_hbm)):
            moves.append((cache_hbm.at[:, 0, :, :, lanes], piece_ref.at[part]))
    moves = fetch(moves, piece_sems)
    for copy in copies:
        copy.wait()
    scale = column(scales_ref[...])
    delta_ref[...] = (codes_ref[...].astype(jnp.float32) * scale).astype(jnp.bfloat16)
    for copy in moves:
        copy.wait()


def cells_of(came_ref, start, size):
    peers, steps, _ = came_ref.shape
    cell = came_ref[:, :, start : start + size].astype(jnp.float32)
    return cell.reshape(peers * steps, size).astype(jnp.bfloat16)


def swap_kernel(came_ref, out_ref):
    _, block, lanes = out_ref.shape
    width = came_ref.shape[2]
    for i in range(2):
        out_ref[i] = cells_of(came_ref, width - (2 - i) * lanes, lanes)


def dot(a, b):
    return jnp.dot(a, b, preferred_element_type=jnp.float32)


def part_kernel(
    came_ref,
    mine_ref,
    other_ref,
    query_hbm,
    pair_hbm,
    queries_ref,
    pairs_ref,
    spread_ref,
    weight_ref,
    sems,
):
    peers, steps, width = came_ref.shape
    features = weight_ref.shape[1]
    rows = queries_ref.shape[1]
    games = rows // steps
    block = peers * steps
    group_index = lax.axis_index("group")
    level = group_index // (SIDES * CORES)
    side, core = lax.rem(group_index // CORES, SIDES), lax.rem(group_index, CORES)
    head = level * KV_HEADS // (peers // CORES)
    pair_rows = features // (peers * SIDES)

    def columns(source, index):
        return source.at[:, pl.ds(pl.multiple_of(index * HEAD, HEAD), HEAD)]

    copies = fetch(
        [
            (columns(query_hbm, (level * SIDES + 0) * CORES + core), weight_ref.at[0]),
            (columns(query_hbm, (level * SIDES + 1) * CORES + core), weight_ref.at[1]),
            (columns(pair_hbm, core * KV_HEADS + head), weight_ref.at[2]),
        ],
        sems,
    )
    inputs = jnp.concatenate(
        [cells_of(came_ref, game * features, features) for game in range(games)], axis=0
    )
    spot = lax.broadcasted_iota(jnp.int32, (1, 2 * block), 1)
    feature = lax.broadcasted_iota(jnp.int32, (features, 2 * block), 0)
    peer, step = spot % block // steps, spot % steps
    offset = jnp.where(spot < block, step, step + steps)
    spreads = []
    for turn in range(SIDES):
        owner = (peer // CORES * SIDES + (side ^ turn)) * CORES + peer % CORES
        source = jnp.where(offset < pair_rows, owner * pair_rows + offset, -1)
        spread = (feature == source).astype(jnp.float32).astype(jnp.bfloat16)
        spreads.append(dot(inputs, spread).astype(jnp.bfloat16))
    spread_ref[...] = spreads[1]
    pairs = dot(spreads[0][:, :block], cells_of(came_ref, width - 2 * LANES, LANES))
    pairs = pairs + dot(spreads[0][:, block:], cells_of(came_ref, width - LANES, LANES))
    mine, other = mine_ref[...], other_ref[...]
    first = dot(inputs, jnp.where(side == 0, mine, other))
    second = dot(inputs, jnp.where(side == 0, other, mine))
    for copy in copies:
        copy.wait()

    def put(ref, i, sums):
        for game in range(games):
            ref[:, game * steps : (game + 1) * steps, i * HEAD : (i + 1) * HEAD] = sums[
                game * block : (game + 1) * block
            ].reshape(peers, steps, HEAD)

    put(queries_ref, 0, first + dot(inputs, weight_ref[0]))
    put(queries_ref, 1, second + dot(inputs, weight_ref[1]))
    put(pairs_ref, 0, pairs + dot(inputs, weight_ref[2]))


def whole_kernel(queries_ref, pairs_ref, spread_ref, other_ref, after1_ref, after2_ref, after3_ref, part_ref):
    peers, rows, wide = queries_ref.shape
    block = spread_ref.shape[1] // 2
    games = spread_ref.shape[0] // block
    steps = rows // games
    part_ref[:, :, :wide] = queries_ref[...]
    pairs = dot(spread_ref[:, :block], other_ref[0]) + dot(spread_ref[:, block:], other_ref[1])
    for game in range(games):
        band = slice(game * steps, (game + 1) * steps)
        part_ref[:, band, wide:] = pairs_ref[:, band, :] + pairs[
            game * block : (game + 1) * block
        ].reshape(peers, steps, HEAD)


def sum_kernel(parts_ref, keep_ref, give_ref):
    core = lax.rem(lax.axis_index("group"), CORES)
    sums = jnp.sum(parts_ref[...], axis=0)
    heads = [sums[:, i * HEAD : (i + 1) * HEAD] for i in range(3)]
    keep_ref[:, :HEAD] = jnp.where(core == 0, heads[0], heads[1]).astype(jnp.bfloat16)
    give_ref[:, :HEAD] = jnp.where(core == 0, heads[1], heads[0]).astype(jnp.bfloat16)
    keep_ref[:, HEAD:] = heads[2].astype(jnp.bfloat16)
    give_ref[:, HEAD:] = heads[2].astype(jnp.bfloat16)


def join_kernel(after_ref, *refs):
    shard_ref = refs[-1]
    for shift, piece_ref in enumerate(refs[:-1]):
        shard_ref[shift] = piece_ref[...]


def facts_kernel(after_ref, named_ref, came_ref, other_ref, placed_ref, ids_ref):
    peers, steps, width = came_ref.shape
    slots, rows = placed_ref.shape
    group_index = lax.axis_index("group")
    side = lax.rem(group_index // CORES, SIDES)
    capacity = slots // (peers * SIDES)

    named = named_ref[...].astype(jnp.float32)
    before = lax.broadcasted_iota(jnp.int32, (rows, rows), 0) < lax.broadcasted_iota(
        jnp.int32, (rows, rows), 1
    )
    rank = jnp.sum(jnp.where((column(named) == named) & before, 1.0, 0.0), axis=0, keepdims=True)
    slot = jnp.where(named >= 0, named * capacity + rank, -1.0)
    index = lax.broadcasted_iota(jnp.int32, (slots, rows), 0).astype(jnp.float32)
    placed_ref[...] = jnp.where(index == slot, 1.0, 0.0).astype(jnp.bfloat16)

    own = came_ref[:, :, width - LANES :].astype(jnp.float32)
    other = other_ref[1].astype(jnp.float32).reshape(own.shape)
    kind = lax.broadcasted_iota(jnp.int32, own.shape, 1) - (steps - 4)
    lane = lax.broadcasted_iota(jnp.int32, (peers, LANES), 1)
    out_lane = lax.broadcasted_iota(jnp.int32, (peers, slots), 1)
    out_peer = lax.broadcasted_iota(jnp.int32, (peers, slots), 0)
    ids = jnp.zeros((peers, slots), jnp.float32)
    for turn, facts in enumerate((own, other)):

        def pick(i):
            return jnp.sum(jnp.where(kind == i, facts, 0.0), axis=1)

        number = pick(0) * 4096.0 + pick(1) * 64.0 + pick(2)
        hit = (pick(3) == group_index.astype(jnp.float32)) & (lane < rows)
        coded = lane.astype(jnp.float32) * 262144.0 + number
        low = jnp.min(jnp.where(hit, coded, 1e9), axis=1, keepdims=True)
        high = jnp.max(jnp.where(hit, coded, -1.0), axis=1, keepdims=True)
        sender = (out_peer // CORES * SIDES + (side ^ turn)) * CORES + out_peer % CORES
        for k, (coded, there) in enumerate(((low, high >= 0), (high, high > low))):
            number = (coded.astype(jnp.int32) & 262143).astype(jnp.float32)
            value = jnp.where(there, number, -1.0)
            ids = ids + jnp.where(out_lane == sender * capacity + k, value, 0.0)
    ids_ref[...] = jnp.sum(ids, axis=0, keepdims=True).astype(jnp.int32)


def attend_kernel(
    lengths_ref,
    mine_ref,
    placed_ref,
    shard0_ref,
    shard1_ref,
    shard2_ref,
    shard3_ref,
    packed_ref,
):
    shards = (shard0_ref, shard1_ref, shard2_ref, shard3_ref)
    count, _, rounds, games, block, _ = shard0_ref.shape
    rows = mine_ref.shape[0]
    steps = rows // games
    heads = CORES
    n_tp = count * len(shards)
    factor = 1.0 / math.sqrt(HEAD)
    mine = mine_ref[...].astype(jnp.float32)
    first, second = mine[:, : 2 * HEAD], mine[:, 2 * HEAD :]
    even = lax.rem(lax.axis_index("tp"), 2) == 0
    with_keys, with_values = jnp.where(even, first, second), jnp.where(even, second, first)
    spot = lax.broadcasted_iota(jnp.int32, (1, count * rounds * block), 1)
    tp_index = lax.axis_index("tp")
    positions = []
    for shift in range(len(shards)):
        across = lax.rem(tp_index, len(shards)) ^ shift
        down = (tp_index // len(shards)) ^ (spot // (rounds * block))
        tp = down * len(shards) + across
        positions.append((spot // block % rounds * n_tp + tp) * block + spot % block)
    contract = (((1,), (1,)), ((), ()))
    games_out = []
    for game in range(games):
        bands = [x[game * steps : (game + 1) * steps] for x in (with_keys, with_values)]
        queries = jnp.concatenate([band[:, :HEAD] for band in bands], axis=0).astype(jnp.bfloat16)
        new_keys, new_values = [band[:, HEAD:].astype(jnp.bfloat16) for band in bands]
        new_scores = factor * lax.dot_general(
            queries, new_keys, contract, preferred_element_type=jnp.float32
        )
        later = lax.broadcasted_iota(jnp.int32, new_scores.shape, 1)
        step = lax.broadcasted_iota(jnp.int32, new_scores.shape, 0) % steps
        new_valid = later <= step
        top = jnp.max(jnp.where(new_valid, new_scores, NEG_FILL), axis=1, keepdims=True)
        kept = []
        for shard_ref, position in zip(shards, positions):
            keys = shard_ref[:, 0, :, game].reshape(count * rounds * block, HEAD)
            scores = factor * lax.dot_general(
                queries, keys, contract, preferred_element_type=jnp.float32
            )
            scores = jnp.where(position < lengths_ref[game], scores, NEG_FILL)
            top = jnp.maximum(top, jnp.max(scores, axis=1, keepdims=True))
            kept.append(scores)
        weight = jnp.where(new_valid, jnp.exp(new_scores - top), 0.0).astype(jnp.bfloat16)
        total = jnp.sum(weight.astype(jnp.float32), axis=1, keepdims=True)
        mixed = jnp.dot(weight, new_values, preferred_element_type=jnp.float32)
        for shard_ref, position, scores in zip(shards, positions, kept):
            values = shard_ref[:, 1, :, game].reshape(count * rounds * block, HEAD)
            weight = jnp.where(
                position < lengths_ref[game], jnp.exp(scores - top), 0.0
            ).astype(jnp.bfloat16)
            total = total + jnp.sum(weight.astype(jnp.float32), axis=1, keepdims=True)
            mixed = mixed + jnp.dot(weight, values, preferred_element_type=jnp.float32)
        out = mixed / total
        games_out.append(
            jnp.concatenate([out[h * steps : (h + 1) * steps] for h in range(heads)], axis=1)
        )
    attended = jnp.concatenate(games_out, axis=0).astype(jnp.bfloat16)
    packed = jnp.dot(placed_ref[...], attended, preferred_element_type=jnp.float32)
    packed_ref[...] = packed.reshape(packed_ref.shape).astype(jnp.bfloat16)


def per_device(
    hidden,
    query_weight,
    key_value_weight,
    query_codes,
    query_scales,
    key_value_codes,
    key_value_scales,
    key_cache,
    value_cache,
    lengths,
    counts,
    learner,
    token_ids,
):
    games, steps, features = hidden.shape
    rows = games * steps
    n_group = lax.axis_size("group")
    n_tp = lax.axis_size("tp")
    peers = n_group // SIDES
    across = n_tp // KV_HEADS
    near = [
        [g for g in range(n_group) if g // CORES % SIDES == side] for side in range(SIDES)
    ]
    turn = []
    for g in range(n_group):
        level, side, core = g // (SIDES * CORES), g // CORES % SIDES, g % CORES
        for t in range(n_tp):
            to = (t // CORES * SIDES + side) * CORES + t % CORES
            turn.append((g * n_tp + t, to * n_tp + level * CORES + core))
    wide = HEADS // n_tp * HEAD
    capacity = max(2, 2 * rows // n_group)
    rounds, _, _, block, _ = key_cache.shape
    pair_rows = key_value_codes.shape[1]
    bf16 = jnp.bfloat16

    def far(x):
        return pltpu.with_memory_space_constraint(x, pltpu.HBM)


    def along(x, axis, shift):
        return lax.ppermute(x, axis, [(i, i ^ shift) for i in range(lax.axis_size(axis))])

    operands = (
        counts.reshape(1, games),
        hidden,
        key_value_codes[0],
        key_value_scales[0].T,
        learner.transpose(0, 2, 1),
        token_ids,
    )
    load, named = pl.pallas_call(
        load_kernel,
        out_shape=[
            jax.ShapeDtypeStruct((peers, steps, games * features + 2 * LANES), bf16),
            jax.ShapeDtypeStruct((1, rows), jnp.int32),
        ],
        grid=(1,),
        in_specs=[whole(x.shape) for x in operands],
        out_specs=[whole((peers, steps, games * features + 2 * LANES)), whole((1, rows))],
        compiler_params=PARAMS,
        name="load",
    )(*[far(x) for x in operands])
    came = lax.all_to_all(
        load, "group", split_axis=0, concat_axis=0, tiled=True, axis_index_groups=near
    )

    piece = jax.ShapeDtypeStruct((2, rounds, games, block, HEAD), bf16)
    query_delta, *pieces = pl.pallas_call(
        pieces_kernel,
        out_shape=[jax.ShapeDtypeStruct(query_codes.shape, bf16)] + [piece] * KV_HEADS,
        in_specs=[HBM] * 4,
        out_specs=[VMEM] * (1 + KV_HEADS),
        scratch_shapes=[
            pltpu.VMEM(query_codes.shape, bf16),
            pltpu.VMEM((1, features), jnp.float32),
            pltpu.SemaphoreType.DMA((2,)),
            pltpu.SemaphoreType.DMA((2 * KV_HEADS,)),
        ],
        compiler_params=PARAMS,
        name="pieces",
    )(far(query_codes), far(query_scales.T), far(key_cache), far(value_cache))
    for shift in range(1, KV_HEADS):
        pieces[shift] = along(pieces[shift], "tp", shift * across)
    query_other = along(query_delta, "group", CORES)
    rows_all = peers * steps
    other = pl.pallas_call(
        swap_kernel,
        out_shape=jax.ShapeDtypeStruct((2, rows_all, LANES), bf16),
        in_specs=[VMEM],
        out_specs=VMEM,
        compiler_params=PARAMS,
        name="swap",
    )(came)
    other = along(other, "group", CORES)

    queries, pairs, spread = pl.pallas_call(
        part_kernel,
        out_shape=[
            jax.ShapeDtypeStruct((peers, rows, wide), jnp.float32),
            jax.ShapeDtypeStruct((peers, rows, HEAD), jnp.float32),
            jax.ShapeDtypeStruct((games * rows_all, 2 * rows_all), bf16),
        ],
        in_specs=[VMEM] * 3 + [HBM] * 2,
        out_specs=[VMEM] * 3,
        scratch_shapes=[
            pltpu.VMEM((3, features, HEAD), bf16),
            pltpu.SemaphoreType.DMA((3,)),
        ],
        compiler_params=PARAMS,
        name="part",
    )(came, query_delta, query_other, far(query_weight), far(key_value_weight))
    part = pl.pallas_call(
        whole_kernel,
        out_shape=jax.ShapeDtypeStruct((peers, rows, wide + HEAD), jnp.float32),
        in_specs=[VMEM] * 4 + [ANY] * 3,
        out_specs=VMEM,
        compiler_params=PARAMS,
        name="whole",
    )(queries, pairs, spread, other, *pieces[1:])
    parts = lax.all_to_all(part, "tp", split_axis=0, concat_axis=0, tiled=True)

    shard = pl.pallas_call(
        join_kernel,
        out_shape=jax.ShapeDtypeStruct((KV_HEADS,) + piece.shape, bf16),
        in_specs=[ANY] + [VMEM] * KV_HEADS,
        out_specs=VMEM,
        compiler_params=PARAMS,
        name="join",
    )(part, *pieces)
    shards = [shard]
    for shift in range(1, across):
        shards.append(along(shard, "tp", shift))
    keep, give = pl.pallas_call(
        sum_kernel,
        out_shape=[jax.ShapeDtypeStruct((rows, 2 * HEAD), bf16)] * 2,
        in_specs=[VMEM],
        out_specs=[VMEM] * 2,
        compiler_params=PARAMS,
        name="sum",
    )(parts)
    got = along(give, "group", 1)
    mine = lax.ppermute(jnp.concatenate([keep, got], axis=1), ("group", "tp"), turn)

    placed, ids_back = pl.pallas_call(
        facts_kernel,
        out_shape=[
            jax.ShapeDtypeStruct((n_group * capacity, rows), bf16),
            jax.ShapeDtypeStruct((1, n_group * capacity), jnp.int32),
        ],
        in_specs=[ANY] + [VMEM] * 3,
        out_specs=[VMEM] * 2,
        compiler_params=PARAMS,
        name="facts",
    )(parts, named, came, other)

    packed = pl.pallas_call(
        attend_kernel,
        out_shape=jax.ShapeDtypeStruct((n_group, capacity, wide), bf16),
        in_specs=[SMEM] + [VMEM] * 6,
        out_specs=VMEM,
        compiler_params=PARAMS,
        name="attend",
    )(lengths, mine, placed, *shards)
    rows_back = lax.all_to_all(packed, "group", split_axis=0, concat_axis=1, tiled=True)
    return (rows_back, ids_back)


def solution(mesh):
    placed = (
        P("group", None, "tp"),
        P("tp", None),
        P("tp", None),
        P("tp", "group"),
        P("tp", "group"),
        P("tp", "group", None),
        P("tp", "group", None),
        P(None, "tp", "group", None, None),
        P(None, "tp", "group", None, None),
        P("group"),
        P("group"),
        P("group", None, None),
        P("group", None),
    )
    return jax.shard_map(
        per_device,
        mesh=mesh,
        in_specs=placed,
        out_specs=(P("group", None, "tp"), P("group", None)),
        check_vma=False,
    )
```

```python
import math

import jax
import jax.numpy as jnp
from jax import lax
from jax.experimental import pallas as pl
from jax.experimental.pallas import tpu as pltpu
from jax.sharding import PartitionSpec as P

HEADS = 32
KV_HEADS = 4
HEAD = 128
CORES = 2
SIDES = 2
LANES = 128


NEG_FILL = -1e30

VMEM = pl.BlockSpec(memory_space=pltpu.VMEM)
SMEM = pl.BlockSpec(memory_space=pltpu.SMEM)
HBM = pl.BlockSpec(memory_space=pltpu.HBM)
ANY = pl.BlockSpec(memory_space=pl.ANY)
PARAMS = pltpu.CompilerParams(vmem_limit_bytes=24 * 1024 * 1024)


def whole(shape):
    return pl.BlockSpec(shape, lambda i: (0,) * len(shape))


def column(row):
    n = row.shape[1]
    across = lax.broadcasted_iota(jnp.int32, (n, n), 1)
    down = lax.broadcasted_iota(jnp.int32, (n, n), 0)
    return jnp.sum(jnp.where(across == down, row, jnp.zeros_like(row)), axis=1, keepdims=True)


def fetch(pairs, sems):
    copies = [
        pltpu.make_async_copy(source, target, sems.at[i]) for i, (source, target) in enumerate(pairs)
    ]
    for copy in copies:
        copy.start()
    return copies


def load_kernel(
    counts_ref, hidden_ref, codes_ref, scales_ref, learner_ref, ids_ref, load_ref, named_ref
):
    peers = load_ref.shape[0]
    games, steps, features = hidden_ref.shape
    inputs = jnp.concatenate(
        [hidden_ref[game].astype(jnp.float32) for game in range(games)], axis=1
    ).astype(jnp.bfloat16)
    load_ref[:, :, : games * features] = jnp.broadcast_to(inputs, (peers,) + inputs.shape)
    step = lax.broadcasted_iota(jnp.int32, (1, steps), 1)
    named = [
        jnp.where(step < counts_ref[:, game : game + 1], learner_ref[game], -1)
        for game in range(games)
    ]
    named = jnp.concatenate(named, axis=1)
    named_ref[...] = named
    ids = jnp.concatenate([ids_ref[game : game + 1] for game in range(games)], axis=1)
    facts = jnp.concatenate([ids >> 12, (ids >> 6) & 63, ids & 63, named], axis=0)
    facts = jnp.concatenate(
        [facts.astype(jnp.float32), jnp.zeros((4, LANES - games * steps), jnp.float32)], axis=1
    )
    extra = codes_ref.shape[0] - steps
    blank = jnp.zeros((steps - 4 - extra, LANES), jnp.float32)
    for block in range(2 * KV_HEADS):
        scale = column(scales_ref[block : block + 1, :])
        delta = codes_ref[:, block * HEAD : (block + 1) * HEAD].astype(jnp.float32) * scale
        rest = jnp.concatenate([delta[steps:], blank, facts], axis=0)
        cell = jnp.concatenate([delta[:steps], rest], axis=1).astype(jnp.bfloat16)
        head, part = block % KV_HEADS, block // KV_HEADS
        for peer in range(part, peers, CORES):
            if peer * KV_HEADS // peers == head:
                load_ref[peer, :, games * features :] = cell


def pieces_kernel(
    codes_hbm,
    scales_hbm,
    key_hbm,
    value_hbm,
    delta_ref,
    piece0_ref,
    piece1_ref,
    piece2_ref,
    piece3_ref,
    codes_ref,
    scales_ref,
    sems,
    piece_sems,
):
    copies = fetch([(codes_hbm, codes_ref), (scales_hbm, scales_ref)], sems)
    own = lax.axis_index("tp") // (lax.axis_size("tp") // KV_HEADS)
    moves = []
    for shift, piece_ref in enumerate((piece0_ref, piece1_ref, piece2_ref, piece3_ref)):
        head = own ^ shift
        lanes = pl.ds(pl.multiple_of(head * HEAD, HEAD), HEAD)
        for part, cache_hbm in enumerate((key_hbm, value_hbm)):
            moves.append((cache_hbm.at[:, 0, :, :, lanes], piece_ref.at[part]))
    moves = fetch(moves, piece_sems)
    for copy in copies:
        copy.wait()
    scale = column(scales_ref[...])
    delta_ref[...] = (codes_ref[...].astype(jnp.float32) * scale).astype(jnp.bfloat16)
    for copy in moves:
        copy.wait()


def cells_of(came_ref, start, size):
    peers, steps, _ = came_ref.shape
    cell = came_ref[:, :, start : start + size].astype(jnp.float32)
    return cell.reshape(peers * steps, size).astype(jnp.bfloat16)


def swap_kernel(came_ref, piece_ref, out_ref, next_ref):
    next_ref[...] = piece_ref[...]
    _, block, lanes = out_ref.shape
    width = came_ref.shape[2]
    for i in range(2):
        out_ref[i] = cells_of(came_ref, width - (2 - i) * lanes, lanes)


def dot(a, b):
    return jnp.dot(a, b, preferred_element_type=jnp.float32)


def part_kernel(
    came_ref,
    mine_ref,
    other_ref,
    query_hbm,
    pair_hbm,
    queries_ref,
    pairs_ref,
    spread_ref,
    weight_ref,
    sems,
):
    peers, steps, width = came_ref.shape
    features = weight_ref.shape[1]
    rows = queries_ref.shape[1]
    games = rows // steps
    block = peers * steps
    group_index = lax.axis_index("group")
    level = group_index // (SIDES * CORES)
    side, core = lax.rem(group_index // CORES, SIDES), lax.rem(group_index, CORES)
    head = level * KV_HEADS // (peers // CORES)
    pair_rows = features // (peers * SIDES)

    def columns(source, index):
        return source.at[:, pl.ds(pl.multiple_of(index * HEAD, HEAD), HEAD)]

    copies = fetch(
        [
            (columns(query_hbm, (level * SIDES + 0) * CORES + core), weight_ref.at[0]),
            (columns(query_hbm, (level * SIDES + 1) * CORES + core), weight_ref.at[1]),
            (columns(pair_hbm, core * KV_HEADS + head), weight_ref.at[2]),
        ],
        sems,
    )
    inputs = jnp.concatenate(
        [cells_of(came_ref, game * features, features) for game in range(games)], axis=0
    )
    spot = lax.broadcasted_iota(jnp.int32, (1, 2 * block), 1)
    feature = lax.broadcasted_iota(jnp.int32, (features, 2 * block), 0)
    peer, step = spot % block // steps, spot % steps
    offset = jnp.where(spot < block, step, step + steps)
    spreads = []
    for turn in range(SIDES):
        owner = (peer // CORES * SIDES + (side ^ turn)) * CORES + peer % CORES
        source = jnp.where(offset < pair_rows, owner * pair_rows + offset, -1)
        spread = (feature == source).astype(jnp.float32).astype(jnp.bfloat16)
        spreads.append(dot(inputs, spread).astype(jnp.bfloat16))
    spread_ref[...] = spreads[1]
    pairs = dot(spreads[0][:, :block], cells_of(came_ref, width - 2 * LANES, LANES))
    pairs = pairs + dot(spreads[0][:, block:], cells_of(came_ref, width - LANES, LANES))
    mine, other = mine_ref[...], other_ref[...]
    first = dot(inputs, jnp.where(side == 0, mine, other))
    second = dot(inputs, jnp.where(side == 0, other, mine))
    for copy in copies:
        copy.wait()

    def put(ref, i, sums):
        for game in range(games):
            ref[:, game * steps : (game + 1) * steps, i * HEAD : (i + 1) * HEAD] = sums[
                game * block : (game + 1) * block
            ].reshape(peers, steps, HEAD)

    put(queries_ref, 0, first + dot(inputs, weight_ref[0]))
    put(queries_ref, 1, second + dot(inputs, weight_ref[1]))
    put(pairs_ref, 0, pairs + dot(inputs, weight_ref[2]))


def whole_kernel(queries_ref, pairs_ref, spread_ref, other_ref, after1_ref, after2_ref, after3_ref, part_ref):
    peers, rows, wide = queries_ref.shape
    block = spread_ref.shape[1] // 2
    games = spread_ref.shape[0] // block
    steps = rows // games
    part_ref[:, :, :wide] = queries_ref[...]
    pairs = dot(spread_ref[:, :block], other_ref[0]) + dot(spread_ref[:, block:], other_ref[1])
    for game in range(games):
        band = slice(game * steps, (game + 1) * steps)
        part_ref[:, band, wide:] = pairs_ref[:, band, :] + pairs[
            game * block : (game + 1) * block
        ].reshape(peers, steps, HEAD)


def sum_kernel(parts_ref, keep_ref, give_ref):
    core = lax.rem(lax.axis_index("group"), CORES)
    sums = jnp.sum(parts_ref[...], axis=0)
    heads = [sums[:, i * HEAD : (i + 1) * HEAD] for i in range(3)]
    keep_ref[:, :HEAD] = jnp.where(core == 0, heads[0], heads[1]).astype(jnp.bfloat16)
    give_ref[:, :HEAD] = jnp.where(core == 0, heads[1], heads[0]).astype(jnp.bfloat16)
    keep_ref[:, HEAD:] = heads[2].astype(jnp.bfloat16)
    give_ref[:, HEAD:] = heads[2].astype(jnp.bfloat16)


def join_kernel(after_ref, *refs):
    shard_ref = refs[-1]
    for shift, piece_ref in enumerate(refs[:-1]):
        shard_ref[shift] = piece_ref[...]


def facts_kernel(after_ref, named_ref, came_ref, other_ref, placed_ref, ids_ref):
    peers, steps, width = came_ref.shape
    slots, rows = placed_ref.shape
    group_index = lax.axis_index("group")
    side = lax.rem(group_index // CORES, SIDES)
    capacity = slots // (peers * SIDES)

    named = named_ref[...].astype(jnp.float32)
    before = lax.broadcasted_iota(jnp.int32, (rows, rows), 0) < lax.broadcasted_iota(
        jnp.int32, (rows, rows), 1
    )
    rank = jnp.sum(jnp.where((column(named) == named) & before, 1.0, 0.0), axis=0, keepdims=True)
    slot = jnp.where(named >= 0, named * capacity + rank, -1.0)
    index = lax.broadcasted_iota(jnp.int32, (slots, rows), 0).astype(jnp.float32)
    placed_ref[...] = jnp.where(index == slot, 1.0, 0.0).astype(jnp.bfloat16)

    own = came_ref[:, :, width - LANES :].astype(jnp.float32)
    other = other_ref[1].astype(jnp.float32).reshape(own.shape)
    kind = lax.broadcasted_iota(jnp.int32, own.shape, 1) - (steps - 4)
    lane = lax.broadcasted_iota(jnp.int32, (peers, LANES), 1)
    out_lane = lax.broadcasted_iota(jnp.int32, (peers, slots), 1)
    out_peer = lax.broadcasted_iota(jnp.int32, (peers, slots), 0)
    ids = jnp.zeros((peers, slots), jnp.float32)
    for turn, facts in enumerate((own, other)):

        def pick(i):
            return jnp.sum(jnp.where(kind == i, facts, 0.0), axis=1)

        number = pick(0) * 4096.0 + pick(1) * 64.0 + pick(2)
        hit = (pick(3) == group_index.astype(jnp.float32)) & (lane < rows)
        coded = lane.astype(jnp.float32) * 262144.0 + number
        low = jnp.min(jnp.where(hit, coded, 1e9), axis=1, keepdims=True)
        high = jnp.max(jnp.where(hit, coded, -1.0), axis=1, keepdims=True)
        sender = (out_peer // CORES * SIDES + (side ^ turn)) * CORES + out_peer % CORES
        for k, (coded, there) in enumerate(((low, high >= 0), (high, high > low))):
            number = (coded.astype(jnp.int32) & 262143).astype(jnp.float32)
            value = jnp.where(there, number, -1.0)
            ids = ids + jnp.where(out_lane == sender * capacity + k, value, 0.0)
    ids_ref[...] = jnp.sum(ids, axis=0, keepdims=True).astype(jnp.int32)


def attend_kernel(
    lengths_ref,
    mine_ref,
    placed_ref,
    shard0_ref,
    shard1_ref,
    shard2_ref,
    shard3_ref,
    packed_ref,
):
    shards = (shard0_ref, shard1_ref, shard2_ref, shard3_ref)
    count, _, rounds, games, block, _ = shard0_ref.shape
    rows = mine_ref.shape[0]
    steps = rows // games
    heads = CORES
    n_tp = count * len(shards)
    factor = 1.0 / math.sqrt(HEAD)
    mine = mine_ref[...].astype(jnp.float32)
    first, second = mine[:, : 2 * HEAD], mine[:, 2 * HEAD :]
    even = lax.rem(lax.axis_index("tp"), 2) == 0
    with_keys, with_values = jnp.where(even, first, second), jnp.where(even, second, first)
    spot = lax.broadcasted_iota(jnp.int32, (1, count * rounds * block), 1)
    tp_index = lax.axis_index("tp")
    positions = []
    for shift in range(len(shards)):
        across = lax.rem(tp_index, len(shards)) ^ shift
        down = (tp_index // len(shards)) ^ (spot // (rounds * block))
        tp = down * len(shards) + across
        positions.append((spot // block % rounds * n_tp + tp) * block + spot % block)
    contract = (((1,), (1,)), ((), ()))
    games_out = []
    for game in range(games):
        bands = [x[game * steps : (game + 1) * steps] for x in (with_keys, with_values)]
        queries = jnp.concatenate([band[:, :HEAD] for band in bands], axis=0).astype(jnp.bfloat16)
        new_keys, new_values = [band[:, HEAD:].astype(jnp.bfloat16) for band in bands]
        new_scores = factor * lax.dot_general(
            queries, new_keys, contract, preferred_element_type=jnp.float32
        )
        later = lax.broadcasted_iota(jnp.int32, new_scores.shape, 1)
        step = lax.broadcasted_iota(jnp.int32, new_scores.shape, 0) % steps
        new_valid = later <= step
        top = jnp.max(jnp.where(new_valid, new_scores, NEG_FILL), axis=1, keepdims=True)
        kept = []
        for shard_ref, position in zip(shards, positions):
            keys = shard_ref[:, 0, :, game].reshape(count * rounds * block, HEAD)
            scores = factor * lax.dot_general(
                queries, keys, contract, preferred_element_type=jnp.float32
            )
            scores = jnp.where(position < lengths_ref[game], scores, NEG_FILL)
            top = jnp.maximum(top, jnp.max(scores, axis=1, keepdims=True))
            kept.append(scores)
        weight = jnp.where(new_valid, jnp.exp(new_scores - top), 0.0).astype(jnp.bfloat16)
        total = jnp.sum(weight.astype(jnp.float32), axis=1, keepdims=True)
        mixed = jnp.dot(weight, new_values, preferred_element_type=jnp.float32)
        for shard_ref, position, scores in zip(shards, positions, kept):
            values = shard_ref[:, 1, :, game].reshape(count * rounds * block, HEAD)
            weight = jnp.where(
                position < lengths_ref[game], jnp.exp(scores - top), 0.0
            ).astype(jnp.bfloat16)
            total = total + jnp.sum(weight.astype(jnp.float32), axis=1, keepdims=True)
            mixed = mixed + jnp.dot(weight, values, preferred_element_type=jnp.float32)
        out = mixed / total
        games_out.append(
            jnp.concatenate([out[h * steps : (h + 1) * steps] for h in range(heads)], axis=1)
        )
    attended = jnp.concatenate(games_out, axis=0).astype(jnp.bfloat16)
    packed = jnp.dot(placed_ref[...], attended, preferred_element_type=jnp.float32)
    packed_ref[...] = packed.reshape(packed_ref.shape).astype(jnp.bfloat16)


def per_device(
    hidden,
    query_weight,
    key_value_weight,
    query_codes,
    query_scales,
    key_value_codes,
    key_value_scales,
    key_cache,
    value_cache,
    lengths,
    counts,
    learner,
    token_ids,
):
    games, steps, features = hidden.shape
    rows = games * steps
    n_group = lax.axis_size("group")
    n_tp = lax.axis_size("tp")
    peers = n_group // SIDES
    across = n_tp // KV_HEADS
    near = [
        [g for g in range(n_group) if g // CORES % SIDES == side] for side in range(SIDES)
    ]
    turn = []
    for g in range(n_group):
        level, side, core = g // (SIDES * CORES), g // CORES % SIDES, g % CORES
        for t in range(n_tp):
            to = (t // CORES * SIDES + side) * CORES + t % CORES
            turn.append((g * n_tp + t, to * n_tp + level * CORES + core))
    wide = HEADS // n_tp * HEAD
    capacity = max(2, 2 * rows // n_group)
    rounds, _, _, block, _ = key_cache.shape
    pair_rows = key_value_codes.shape[1]
    bf16 = jnp.bfloat16

    def far(x):
        return pltpu.with_memory_space_constraint(x, pltpu.HBM)


    def along(x, axis, shift):
        return lax.ppermute(x, axis, [(i, i ^ shift) for i in range(lax.axis_size(axis))])

    operands = (
        counts.reshape(1, games),
        hidden,
        key_value_codes[0],
        key_value_scales[0].T,
        learner.transpose(0, 2, 1),
        token_ids,
    )
    load, named = pl.pallas_call(
        load_kernel,
        out_shape=[
            jax.ShapeDtypeStruct((peers, steps, games * features + 2 * LANES), bf16),
            jax.ShapeDtypeStruct((1, rows), jnp.int32),
        ],
        grid=(1,),
        in_specs=[whole(x.shape) for x in operands],
        out_specs=[whole((peers, steps, games * features + 2 * LANES)), whole((1, rows))],
        compiler_params=PARAMS,
        name="load",
    )(*[far(x) for x in operands])
    came = lax.all_to_all(
        load, "group", split_axis=0, concat_axis=0, tiled=True, axis_index_groups=near
    )

    piece = jax.ShapeDtypeStruct((2, rounds, games, block, HEAD), bf16)
    query_delta, *pieces = pl.pallas_call(
        pieces_kernel,
        out_shape=[jax.ShapeDtypeStruct(query_codes.shape, bf16)] + [piece] * KV_HEADS,
        in_specs=[HBM] * 4,
        out_specs=[VMEM] * (1 + KV_HEADS),
        scratch_shapes=[
            pltpu.VMEM(query_codes.shape, bf16),
            pltpu.VMEM((1, features), jnp.float32),
            pltpu.SemaphoreType.DMA((2,)),
            pltpu.SemaphoreType.DMA((2 * KV_HEADS,)),
        ],
        compiler_params=PARAMS,
        name="pieces",
    )(far(query_codes), far(query_scales.T), far(key_cache), far(value_cache))
    for shift in range(2, KV_HEADS):
        pieces[shift] = along(pieces[shift], "tp", shift * across)
    query_other = along(query_delta, "group", CORES)
    rows_all = peers * steps
    other, later = pl.pallas_call(
        swap_kernel,
        out_shape=[jax.ShapeDtypeStruct((2, rows_all, LANES), bf16), piece],
        in_specs=[VMEM] * 2,
        out_specs=[VMEM] * 2,
        compiler_params=PARAMS,
        name="swap",
    )(came, pieces[1])
    other = along(other, "group", CORES)
    pieces[1] = along(later, "tp", across)

    queries, pairs, spread = pl.pallas_call(
        part_kernel,
        out_shape=[
            jax.ShapeDtypeStruct((peers, rows, wide), jnp.float32),
            jax.ShapeDtypeStruct((peers, rows, HEAD), jnp.float32),
            jax.ShapeDtypeStruct((games * rows_all, 2 * rows_all), bf16),
        ],
        in_specs=[VMEM] * 3 + [HBM] * 2,
        out_specs=[VMEM] * 3,
        scratch_shapes=[
            pltpu.VMEM((3, features, HEAD), bf16),
            pltpu.SemaphoreType.DMA((3,)),
        ],
        compiler_params=PARAMS,
        name="part",
    )(came, query_delta, query_other, far(query_weight), far(key_value_weight))
    part = pl.pallas_call(
        whole_kernel,
        out_shape=jax.ShapeDtypeStruct((peers, rows, wide + HEAD), jnp.float32),
        in_specs=[VMEM] * 4 + [ANY] * 3,
        out_specs=VMEM,
        compiler_params=PARAMS,
        name="whole",
    )(queries, pairs, spread, other, *pieces[1:])
    parts = lax.all_to_all(part, "tp", split_axis=0, concat_axis=0, tiled=True)

    shard = pl.pallas_call(
        join_kernel,
        out_shape=jax.ShapeDtypeStruct((KV_HEADS,) + piece.shape, bf16),
        in_specs=[ANY] + [VMEM] * KV_HEADS,
        out_specs=VMEM,
        compiler_params=PARAMS,
        name="join",
    )(part, *pieces)
    shards = [shard]
    for shift in range(1, across):
        shards.append(along(shard, "tp", shift))
    keep, give = pl.pallas_call(
        sum_kernel,
        out_shape=[jax.ShapeDtypeStruct((rows, 2 * HEAD), bf16)] * 2,
        in_specs=[VMEM],
        out_specs=[VMEM] * 2,
        compiler_params=PARAMS,
        name="sum",
    )(parts)
    got = along(give, "group", 1)
    mine = lax.ppermute(jnp.concatenate([keep, got], axis=1), ("group", "tp"), turn)

    placed, ids_back = pl.pallas_call(
        facts_kernel,
        out_shape=[
            jax.ShapeDtypeStruct((n_group * capacity, rows), bf16),
            jax.ShapeDtypeStruct((1, n_group * capacity), jnp.int32),
        ],
        in_specs=[ANY] + [VMEM] * 3,
        out_specs=[VMEM] * 2,
        compiler_params=PARAMS,
        name="facts",
    )(parts, named, came, other)

    packed = pl.pallas_call(
        attend_kernel,
        out_shape=jax.ShapeDtypeStruct((n_group, capacity, wide), bf16),
        in_specs=[SMEM] + [VMEM] * 6,
        out_specs=VMEM,
        compiler_params=PARAMS,
        name="attend",
    )(lengths, mine, placed, *shards)
    rows_back = lax.all_to_all(packed, "group", split_axis=0, concat_axis=1, tiled=True)
    return (rows_back, ids_back)


def solution(mesh):
    placed = (
        P("group", None, "tp"),
        P("tp", None),
        P("tp", None),
        P("tp", "group"),
        P("tp", "group"),
        P("tp", "group", None),
        P("tp", "group", None),
        P(None, "tp", "group", None, None),
        P(None, "tp", "group", None, None),
        P("group"),
        P("group"),
        P("group", None, None),
        P("group", None),
    )
    return jax.shard_map(
        per_device,
        mesh=mesh,
        in_specs=placed,
        out_specs=(P("group", None, "tp"), P("group", None)),
        check_vma=False,
    )
```

```python
import math

import jax
import jax.numpy as jnp
from jax import lax
from jax.experimental import pallas as pl
from jax.experimental.pallas import tpu as pltpu
from jax.sharding import PartitionSpec as P

HEADS = 32
KV_HEADS = 4
HEAD = 128
CORES = 2
SIDES = 2
LANES = 128


NEG_FILL = -1e30

VMEM = pl.BlockSpec(memory_space=pltpu.VMEM)
SMEM = pl.BlockSpec(memory_space=pltpu.SMEM)
HBM = pl.BlockSpec(memory_space=pltpu.HBM)
ANY = pl.BlockSpec(memory_space=pl.ANY)
PARAMS = pltpu.CompilerParams(vmem_limit_bytes=24 * 1024 * 1024)


def whole(shape):
    return pl.BlockSpec(shape, lambda i: (0,) * len(shape))


def column(row):
    n = row.shape[1]
    across = lax.broadcasted_iota(jnp.int32, (n, n), 1)
    down = lax.broadcasted_iota(jnp.int32, (n, n), 0)
    return jnp.sum(jnp.where(across == down, row, jnp.zeros_like(row)), axis=1, keepdims=True)


def fetch(pairs, sems):
    copies = [
        pltpu.make_async_copy(source, target, sems.at[i]) for i, (source, target) in enumerate(pairs)
    ]
    for copy in copies:
        copy.start()
    return copies


def load_kernel(
    counts_ref, hidden_ref, codes_ref, scales_ref, learner_ref, ids_ref, load_ref, named_ref
):
    peers = load_ref.shape[0]
    games, steps, features = hidden_ref.shape
    inputs = jnp.concatenate(
        [hidden_ref[game].astype(jnp.float32) for game in range(games)], axis=1
    ).astype(jnp.bfloat16)
    load_ref[:, :, : games * features] = jnp.broadcast_to(inputs, (peers,) + inputs.shape)
    step = lax.broadcasted_iota(jnp.int32, (1, steps), 1)
    named = [
        jnp.where(step < counts_ref[:, game : game + 1], learner_ref[game], -1)
        for game in range(games)
    ]
    named = jnp.concatenate(named, axis=1)
    named_ref[...] = named
    ids = jnp.concatenate([ids_ref[game : game + 1] for game in range(games)], axis=1)
    facts = jnp.concatenate([ids >> 12, (ids >> 6) & 63, ids & 63, named], axis=0)
    facts = jnp.concatenate(
        [facts.astype(jnp.float32), jnp.zeros((4, LANES - games * steps), jnp.float32)], axis=1
    )
    extra = codes_ref.shape[0] - steps
    blank = jnp.zeros((steps - 4 - extra, LANES), jnp.float32)
    for block in range(2 * KV_HEADS):
        scale = column(scales_ref[block : block + 1, :])
        delta = codes_ref[:, block * HEAD : (block + 1) * HEAD].astype(jnp.float32) * scale
        rest = jnp.concatenate([delta[steps:], blank, facts], axis=0)
        cell = jnp.concatenate([delta[:steps], rest], axis=1).astype(jnp.bfloat16)
        head, part = block % KV_HEADS, block // KV_HEADS
        for peer in range(part, peers, CORES):
            if peer * KV_HEADS // peers == head:
                load_ref[peer, :, games * features :] = cell


def pieces_kernel(
    codes_hbm,
    scales_hbm,
    key_hbm,
    value_hbm,
    delta_ref,
    piece0_ref,
    piece1_ref,
    piece2_ref,
    piece3_ref,
    codes_ref,
    scales_ref,
    sems,
    piece_sems,
):
    copies = fetch([(codes_hbm, codes_ref), (scales_hbm, scales_ref)], sems)
    own = lax.axis_index("tp") // (lax.axis_size("tp") // KV_HEADS)
    moves = []
    for shift, piece_ref in enumerate((piece0_ref, piece1_ref, piece2_ref, piece3_ref)):
        head = own ^ shift
        lanes = pl.ds(pl.multiple_of(head * HEAD, HEAD), HEAD)
        for part, cache_hbm in enumerate((key_hbm, value_hbm)):
            moves.append((cache_hbm.at[:, 0, :, :, lanes], piece_ref.at[part]))
    moves = fetch(moves, piece_sems)
    for copy in copies:
        copy.wait()
    scale = column(scales_ref[...])
    delta_ref[...] = (codes_ref[...].astype(jnp.float32) * scale).astype(jnp.bfloat16)
    for copy in moves:
        copy.wait()


def cells_of(came_ref, start, size):
    peers, steps, _ = came_ref.shape
    cell = came_ref[:, :, start : start + size].astype(jnp.float32)
    return cell.reshape(peers * steps, size).astype(jnp.bfloat16)


def swap_kernel(came_ref, piece2_ref, piece1_ref, out_ref, next2_ref, next1_ref):
    next2_ref[...] = piece2_ref[...]
    next1_ref[...] = piece1_ref[...]
    _, block, lanes = out_ref.shape
    width = came_ref.shape[2]
    for i in range(2):
        out_ref[i] = cells_of(came_ref, width - (2 - i) * lanes, lanes)


def dot(a, b):
    return jnp.dot(a, b, preferred_element_type=jnp.float32)


def part_kernel(
    came_ref,
    mine_ref,
    other_ref,
    query_hbm,
    pair_hbm,
    queries_ref,
    pairs_ref,
    spread_ref,
    weight_ref,
    sems,
):
    peers, steps, width = came_ref.shape
    features = weight_ref.shape[1]
    rows = queries_ref.shape[1]
    games = rows // steps
    block = peers * steps
    group_index = lax.axis_index("group")
    level = group_index // (SIDES * CORES)
    side, core = lax.rem(group_index // CORES, SIDES), lax.rem(group_index, CORES)
    head = level * KV_HEADS // (peers // CORES)
    pair_rows = features // (peers * SIDES)

    def columns(source, index):
        return source.at[:, pl.ds(pl.multiple_of(index * HEAD, HEAD), HEAD)]

    copies = fetch(
        [
            (columns(query_hbm, (level * SIDES + 0) * CORES + core), weight_ref.at[0]),
            (columns(query_hbm, (level * SIDES + 1) * CORES + core), weight_ref.at[1]),
            (columns(pair_hbm, core * KV_HEADS + head), weight_ref.at[2]),
        ],
        sems,
    )
    inputs = jnp.concatenate(
        [cells_of(came_ref, game * features, features) for game in range(games)], axis=0
    )
    spot = lax.broadcasted_iota(jnp.int32, (1, 2 * block), 1)
    feature = lax.broadcasted_iota(jnp.int32, (features, 2 * block), 0)
    peer, step = spot % block // steps, spot % steps
    offset = jnp.where(spot < block, step, step + steps)
    spreads = []
    for turn in range(SIDES):
        owner = (peer // CORES * SIDES + (side ^ turn)) * CORES + peer % CORES
        source = jnp.where(offset < pair_rows, owner * pair_rows + offset, -1)
        spread = (feature == source).astype(jnp.float32).astype(jnp.bfloat16)
        spreads.append(dot(inputs, spread).astype(jnp.bfloat16))
    spread_ref[...] = spreads[1]
    pairs = dot(spreads[0][:, :block], cells_of(came_ref, width - 2 * LANES, LANES))
    pairs = pairs + dot(spreads[0][:, block:], cells_of(came_ref, width - LANES, LANES))
    mine, other = mine_ref[...], other_ref[...]
    first = dot(inputs, jnp.where(side == 0, mine, other))
    second = dot(inputs, jnp.where(side == 0, other, mine))
    for copy in copies:
        copy.wait()

    def put(ref, i, sums):
        for game in range(games):
            ref[:, game * steps : (game + 1) * steps, i * HEAD : (i + 1) * HEAD] = sums[
                game * block : (game + 1) * block
            ].reshape(peers, steps, HEAD)

    put(queries_ref, 0, first + dot(inputs, weight_ref[0]))
    put(queries_ref, 1, second + dot(inputs, weight_ref[1]))
    put(pairs_ref, 0, pairs + dot(inputs, weight_ref[2]))


def whole_kernel(queries_ref, pairs_ref, spread_ref, other_ref, after1_ref, after2_ref, after3_ref, part_ref):
    peers, rows, wide = queries_ref.shape
    block = spread_ref.shape[1] // 2
    games = spread_ref.shape[0] // block
    steps = rows // games
    part_ref[:, :, :wide] = queries_ref[...]
    pairs = dot(spread_ref[:, :block], other_ref[0]) + dot(spread_ref[:, block:], other_ref[1])
    for game in range(games):
        band = slice(game * steps, (game + 1) * steps)
        part_ref[:, band, wide:] = pairs_ref[:, band, :] + pairs[
            game * block : (game + 1) * block
        ].reshape(peers, steps, HEAD)


def sum_kernel(parts_ref, keep_ref, give_ref):
    core = lax.rem(lax.axis_index("group"), CORES)
    sums = jnp.sum(parts_ref[...], axis=0)
    heads = [sums[:, i * HEAD : (i + 1) * HEAD] for i in range(3)]
    keep_ref[:, :HEAD] = jnp.where(core == 0, heads[0], heads[1]).astype(jnp.bfloat16)
    give_ref[:, :HEAD] = jnp.where(core == 0, heads[1], heads[0]).astype(jnp.bfloat16)
    keep_ref[:, HEAD:] = heads[2].astype(jnp.bfloat16)
    give_ref[:, HEAD:] = heads[2].astype(jnp.bfloat16)


def join_kernel(after_ref, *refs):
    shard_ref = refs[-1]
    for shift, piece_ref in enumerate(refs[:-1]):
        shard_ref[shift] = piece_ref[...]


def facts_kernel(after_ref, named_ref, came_ref, other_ref, placed_ref, ids_ref):
    peers, steps, width = came_ref.shape
    slots, rows = placed_ref.shape
    group_index = lax.axis_index("group")
    side = lax.rem(group_index // CORES, SIDES)
    capacity = slots // (peers * SIDES)

    named = named_ref[...].astype(jnp.float32)
    before = lax.broadcasted_iota(jnp.int32, (rows, rows), 0) < lax.broadcasted_iota(
        jnp.int32, (rows, rows), 1
    )
    rank = jnp.sum(jnp.where((column(named) == named) & before, 1.0, 0.0), axis=0, keepdims=True)
    slot = jnp.where(named >= 0, named * capacity + rank, -1.0)
    index = lax.broadcasted_iota(jnp.int32, (slots, rows), 0).astype(jnp.float32)
    placed_ref[...] = jnp.where(index == slot, 1.0, 0.0).astype(jnp.bfloat16)

    own = came_ref[:, :, width - LANES :].astype(jnp.float32)
    other = other_ref[1].astype(jnp.float32).reshape(own.shape)
    kind = lax.broadcasted_iota(jnp.int32, own.shape, 1) - (steps - 4)
    lane = lax.broadcasted_iota(jnp.int32, (peers, LANES), 1)
    out_lane = lax.broadcasted_iota(jnp.int32, (peers, slots), 1)
    out_peer = lax.broadcasted_iota(jnp.int32, (peers, slots), 0)
    ids = jnp.zeros((peers, slots), jnp.float32)
    for turn, facts in enumerate((own, other)):

        def pick(i):
            return jnp.sum(jnp.where(kind == i, facts, 0.0), axis=1)

        number = pick(0) * 4096.0 + pick(1) * 64.0 + pick(2)
        hit = (pick(3) == group_index.astype(jnp.float32)) & (lane < rows)
        coded = lane.astype(jnp.float32) * 262144.0 + number
        low = jnp.min(jnp.where(hit, coded, 1e9), axis=1, keepdims=True)
        high = jnp.max(jnp.where(hit, coded, -1.0), axis=1, keepdims=True)
        sender = (out_peer // CORES * SIDES + (side ^ turn)) * CORES + out_peer % CORES
        for k, (coded, there) in enumerate(((low, high >= 0), (high, high > low))):
            number = (coded.astype(jnp.int32) & 262143).astype(jnp.float32)
            value = jnp.where(there, number, -1.0)
            ids = ids + jnp.where(out_lane == sender * capacity + k, value, 0.0)
    ids_ref[...] = jnp.sum(ids, axis=0, keepdims=True).astype(jnp.int32)


def attend_kernel(
    lengths_ref,
    mine_ref,
    placed_ref,
    shard0_ref,
    shard1_ref,
    shard2_ref,
    shard3_ref,
    packed_ref,
):
    shards = (shard0_ref, shard1_ref, shard2_ref, shard3_ref)
    count, _, rounds, games, block, _ = shard0_ref.shape
    rows = mine_ref.shape[0]
    steps = rows // games
    heads = CORES
    n_tp = count * len(shards)
    factor = 1.0 / math.sqrt(HEAD)
    mine = mine_ref[...].astype(jnp.float32)
    first, second = mine[:, : 2 * HEAD], mine[:, 2 * HEAD :]
    even = lax.rem(lax.axis_index("tp"), 2) == 0
    with_keys, with_values = jnp.where(even, first, second), jnp.where(even, second, first)
    spot = lax.broadcasted_iota(jnp.int32, (1, count * rounds * block), 1)
    tp_index = lax.axis_index("tp")
    positions = []
    for shift in range(len(shards)):
        across = lax.rem(tp_index, len(shards)) ^ shift
        down = (tp_index // len(shards)) ^ (spot // (rounds * block))
        tp = down * len(shards) + across
        positions.append((spot // block % rounds * n_tp + tp) * block + spot % block)
    contract = (((1,), (1,)), ((), ()))
    games_out = []
    for game in range(games):
        bands = [x[game * steps : (game + 1) * steps] for x in (with_keys, with_values)]
        queries = jnp.concatenate([band[:, :HEAD] for band in bands], axis=0).astype(jnp.bfloat16)
        new_keys, new_values = [band[:, HEAD:].astype(jnp.bfloat16) for band in bands]
        new_scores = factor * lax.dot_general(
            queries, new_keys, contract, preferred_element_type=jnp.float32
        )
        later = lax.broadcasted_iota(jnp.int32, new_scores.shape, 1)
        step = lax.broadcasted_iota(jnp.int32, new_scores.shape, 0) % steps
        new_valid = later <= step
        top = jnp.max(jnp.where(new_valid, new_scores, NEG_FILL), axis=1, keepdims=True)
        kept = []
        for shard_ref, position in zip(shards, positions):
            keys = shard_ref[:, 0, :, game].reshape(count * rounds * block, HEAD)
            scores = factor * lax.dot_general(
                queries, keys, contract, preferred_element_type=jnp.float32
            )
            scores = jnp.where(position < lengths_ref[game], scores, NEG_FILL)
            top = jnp.maximum(top, jnp.max(scores, axis=1, keepdims=True))
            kept.append(scores)
        weight = jnp.where(new_valid, jnp.exp(new_scores - top), 0.0).astype(jnp.bfloat16)
        total = jnp.sum(weight.astype(jnp.float32), axis=1, keepdims=True)
        mixed = jnp.dot(weight, new_values, preferred_element_type=jnp.float32)
        for shard_ref, position, scores in zip(shards, positions, kept):
            values = shard_ref[:, 1, :, game].reshape(count * rounds * block, HEAD)
            weight = jnp.where(
                position < lengths_ref[game], jnp.exp(scores - top), 0.0
            ).astype(jnp.bfloat16)
            total = total + jnp.sum(weight.astype(jnp.float32), axis=1, keepdims=True)
            mixed = mixed + jnp.dot(weight, values, preferred_element_type=jnp.float32)
        out = mixed / total
        games_out.append(
            jnp.concatenate([out[h * steps : (h + 1) * steps] for h in range(heads)], axis=1)
        )
    attended = jnp.concatenate(games_out, axis=0).astype(jnp.bfloat16)
    packed = jnp.dot(placed_ref[...], attended, preferred_element_type=jnp.float32)
    packed_ref[...] = packed.reshape(packed_ref.shape).astype(jnp.bfloat16)


def per_device(
    hidden,
    query_weight,
    key_value_weight,
    query_codes,
    query_scales,
    key_value_codes,
    key_value_scales,
    key_cache,
    value_cache,
    lengths,
    counts,
    learner,
    token_ids,
):
    games, steps, features = hidden.shape
    rows = games * steps
    n_group = lax.axis_size("group")
    n_tp = lax.axis_size("tp")
    peers = n_group // SIDES
    across = n_tp // KV_HEADS
    near = [
        [g for g in range(n_group) if g // CORES % SIDES == side] for side in range(SIDES)
    ]
    turn = []
    for g in range(n_group):
        level, side, core = g // (SIDES * CORES), g // CORES % SIDES, g % CORES
        for t in range(n_tp):
            to = (t // CORES * SIDES + side) * CORES + t % CORES
            turn.append((g * n_tp + t, to * n_tp + level * CORES + core))
    wide = HEADS // n_tp * HEAD
    capacity = max(2, 2 * rows // n_group)
    rounds, _, _, block, _ = key_cache.shape
    pair_rows = key_value_codes.shape[1]
    bf16 = jnp.bfloat16

    def far(x):
        return pltpu.with_memory_space_constraint(x, pltpu.HBM)


    def along(x, axis, shift):
        return lax.ppermute(x, axis, [(i, i ^ shift) for i in range(lax.axis_size(axis))])

    operands = (
        counts.reshape(1, games),
        hidden,
        key_value_codes[0],
        key_value_scales[0].T,
        learner.transpose(0, 2, 1),
        token_ids,
    )
    load, named = pl.pallas_call(
        load_kernel,
        out_shape=[
            jax.ShapeDtypeStruct((peers, steps, games * features + 2 * LANES), bf16),
            jax.ShapeDtypeStruct((1, rows), jnp.int32),
        ],
        grid=(1,),
        in_specs=[whole(x.shape) for x in operands],
        out_specs=[whole((peers, steps, games * features + 2 * LANES)), whole((1, rows))],
        compiler_params=PARAMS,
        name="load",
    )(*[far(x) for x in operands])
    came = lax.all_to_all(
        load, "group", split_axis=0, concat_axis=0, tiled=True, axis_index_groups=near
    )

    piece = jax.ShapeDtypeStruct((2, rounds, games, block, HEAD), bf16)
    query_delta, *pieces = pl.pallas_call(
        pieces_kernel,
        out_shape=[jax.ShapeDtypeStruct(query_codes.shape, bf16)] + [piece] * KV_HEADS,
        in_specs=[HBM] * 4,
        out_specs=[VMEM] * (1 + KV_HEADS),
        scratch_shapes=[
            pltpu.VMEM(query_codes.shape, bf16),
            pltpu.VMEM((1, features), jnp.float32),
            pltpu.SemaphoreType.DMA((2,)),
            pltpu.SemaphoreType.DMA((2 * KV_HEADS,)),
        ],
        compiler_params=PARAMS,
        name="pieces",
    )(far(query_codes), far(query_scales.T), far(key_cache), far(value_cache))
    pieces[3] = along(pieces[3], "tp", 3 * across)
    query_other = along(query_delta, "group", CORES)
    rows_all = peers * steps
    other, *later = pl.pallas_call(
        swap_kernel,
        out_shape=[jax.ShapeDtypeStruct((2, rows_all, LANES), bf16), piece, piece],
        in_specs=[VMEM] * 3,
        out_specs=[VMEM] * 3,
        compiler_params=PARAMS,
        name="swap",
    )(came, pieces[2], pieces[1])
    other = along(other, "group", CORES)
    pieces[2] = along(later[0], "tp", 2 * across)
    pieces[1] = along(later[1], "tp", across)

    queries, pairs, spread = pl.pallas_call(
        part_kernel,
        out_shape=[
            jax.ShapeDtypeStruct((peers, rows, wide), jnp.float32),
            jax.ShapeDtypeStruct((peers, rows, HEAD), jnp.float32),
            jax.ShapeDtypeStruct((games * rows_all, 2 * rows_all), bf16),
        ],
        in_specs=[VMEM] * 3 + [HBM] * 2,
        out_specs=[VMEM] * 3,
        scratch_shapes=[
            pltpu.VMEM((3, features, HEAD), bf16),
            pltpu.SemaphoreType.DMA((3,)),
        ],
        compiler_params=PARAMS,
        name="part",
    )(came, query_delta, query_other, far(query_weight), far(key_value_weight))
    part = pl.pallas_call(
        whole_kernel,
        out_shape=jax.ShapeDtypeStruct((peers, rows, wide + HEAD), jnp.float32),
        in_specs=[VMEM] * 4 + [ANY] * 3,
        out_specs=VMEM,
        compiler_params=PARAMS,
        name="whole",
    )(queries, pairs, spread, other, *pieces[1:])
    parts = lax.all_to_all(part, "tp", split_axis=0, concat_axis=0, tiled=True)

    shard = pl.pallas_call(
        join_kernel,
        out_shape=jax.ShapeDtypeStruct((KV_HEADS,) + piece.shape, bf16),
        in_specs=[ANY] + [VMEM] * KV_HEADS,
        out_specs=VMEM,
        compiler_params=PARAMS,
        name="join",
    )(part, *pieces)
    shards = [shard]
    for shift in range(1, across):
        shards.append(along(shard, "tp", shift))
    keep, give = pl.pallas_call(
        sum_kernel,
        out_shape=[jax.ShapeDtypeStruct((rows, 2 * HEAD), bf16)] * 2,
        in_specs=[VMEM],
        out_specs=[VMEM] * 2,
        compiler_params=PARAMS,
        name="sum",
    )(parts)
    got = along(give, "group", 1)
    mine = lax.ppermute(jnp.concatenate([keep, got], axis=1), ("group", "tp"), turn)

    placed, ids_back = pl.pallas_call(
        facts_kernel,
        out_shape=[
            jax.ShapeDtypeStruct((n_group * capacity, rows), bf16),
            jax.ShapeDtypeStruct((1, n_group * capacity), jnp.int32),
        ],
        in_specs=[ANY] + [VMEM] * 3,
        out_specs=[VMEM] * 2,
        compiler_params=PARAMS,
        name="facts",
    )(parts, named, came, other)

    packed = pl.pallas_call(
        attend_kernel,
        out_shape=jax.ShapeDtypeStruct((n_group, capacity, wide), bf16),
        in_specs=[SMEM] + [VMEM] * 6,
        out_specs=VMEM,
        compiler_params=PARAMS,
        name="attend",
    )(lengths, mine, placed, *shards)
    rows_back = lax.all_to_all(packed, "group", split_axis=0, concat_axis=1, tiled=True)
    return (rows_back, ids_back)


def solution(mesh):
    placed = (
        P("group", None, "tp"),
        P("tp", None),
        P("tp", None),
        P("tp", "group"),
        P("tp", "group"),
        P("tp", "group", None),
        P("tp", "group", None),
        P(None, "tp", "group", None, None),
        P(None, "tp", "group", None, None),
        P("group"),
        P("group"),
        P("group", None, None),
        P("group", None),
    )
    return jax.shard_map(
        per_device,
        mesh=mesh,
        in_specs=placed,
        out_specs=(P("group", None, "tp"), P("group", None)),
        check_vma=False,
    )
```

```python
import math

import jax
import jax.numpy as jnp
from jax import lax
from jax.experimental import pallas as pl
from jax.experimental.pallas import tpu as pltpu
from jax.sharding import PartitionSpec as P

HEADS = 32
KV_HEADS = 4
HEAD = 128
CORES = 2
SIDES = 2
LANES = 128


NEG_FILL = -1e30

VMEM = pl.BlockSpec(memory_space=pltpu.VMEM)
SMEM = pl.BlockSpec(memory_space=pltpu.SMEM)
HBM = pl.BlockSpec(memory_space=pltpu.HBM)
ANY = pl.BlockSpec(memory_space=pl.ANY)
PARAMS = pltpu.CompilerParams(vmem_limit_bytes=24 * 1024 * 1024)


def whole(shape):
    return pl.BlockSpec(shape, lambda i: (0,) * len(shape))


def column(row):
    n = row.shape[1]
    across = lax.broadcasted_iota(jnp.int32, (n, n), 1)
    down = lax.broadcasted_iota(jnp.int32, (n, n), 0)
    return jnp.sum(jnp.where(across == down, row, jnp.zeros_like(row)), axis=1, keepdims=True)


def fetch(pairs, sems):
    copies = [
        pltpu.make_async_copy(source, target, sems.at[i]) for i, (source, target) in enumerate(pairs)
    ]
    for copy in copies:
        copy.start()
    return copies


def load_kernel(
    counts_ref, hidden_ref, codes_ref, scales_ref, learner_ref, ids_ref, load_ref, named_ref
):
    peers = load_ref.shape[0]
    games, steps, features = hidden_ref.shape
    inputs = jnp.concatenate(
        [hidden_ref[game].astype(jnp.float32) for game in range(games)], axis=1
    ).astype(jnp.bfloat16)
    load_ref[:, :, : games * features] = jnp.broadcast_to(inputs, (peers,) + inputs.shape)
    step = lax.broadcasted_iota(jnp.int32, (1, steps), 1)
    named = [
        jnp.where(step < counts_ref[:, game : game + 1], learner_ref[game], -1)
        for game in range(games)
    ]
    named = jnp.concatenate(named, axis=1)
    named_ref[...] = named
    ids = jnp.concatenate([ids_ref[game : game + 1] for game in range(games)], axis=1)
    facts = jnp.concatenate([ids >> 12, (ids >> 6) & 63, ids & 63, named], axis=0)
    facts = jnp.concatenate(
        [facts.astype(jnp.float32), jnp.zeros((4, LANES - games * steps), jnp.float32)], axis=1
    )
    extra = codes_ref.shape[0] - steps
    blank = jnp.zeros((steps - 4 - extra, LANES), jnp.float32)
    for block in range(2 * KV_HEADS):
        scale = column(scales_ref[block : block + 1, :])
        delta = codes_ref[:, block * HEAD : (block + 1) * HEAD].astype(jnp.float32) * scale
        rest = jnp.concatenate([delta[steps:], blank, facts], axis=0)
        cell = jnp.concatenate([delta[:steps], rest], axis=1).astype(jnp.bfloat16)
        head, part = block % KV_HEADS, block // KV_HEADS
        for peer in range(part, peers, CORES):
            if peer * KV_HEADS // peers == head:
                load_ref[peer, :, games * features :] = cell


def pieces_kernel(
    codes_hbm,
    scales_hbm,
    key_hbm,
    value_hbm,
    delta_ref,
    piece0_ref,
    piece1_ref,
    piece2_ref,
    piece3_ref,
    codes_ref,
    scales_ref,
    sems,
    piece_sems,
):
    copies = fetch([(codes_hbm, codes_ref), (scales_hbm, scales_ref)], sems)
    own = lax.axis_index("tp") // (lax.axis_size("tp") // KV_HEADS)
    moves = []
    for shift, piece_ref in enumerate((piece0_ref, piece1_ref, piece2_ref, piece3_ref)):
        head = own ^ shift
        lanes = pl.ds(pl.multiple_of(head * HEAD, HEAD), HEAD)
        for part, cache_hbm in enumerate((key_hbm, value_hbm)):
            moves.append((cache_hbm.at[:, 0, :, :, lanes], piece_ref.at[part]))
    moves = fetch(moves, piece_sems)
    for copy in copies:
        copy.wait()
    scale = column(scales_ref[...])
    delta_ref[...] = (codes_ref[...].astype(jnp.float32) * scale).astype(jnp.bfloat16)
    for copy in moves:
        copy.wait()


def cells_of(came_ref, start, size):
    peers, steps, _ = came_ref.shape
    cell = came_ref[:, :, start : start + size].astype(jnp.float32)
    return cell.reshape(peers * steps, size).astype(jnp.bfloat16)


def swap_kernel(came_ref, piece_ref, out_ref, next_ref):
    next_ref[...] = piece_ref[...]
    _, block, lanes = out_ref.shape
    width = came_ref.shape[2]
    for i in range(2):
        out_ref[i] = cells_of(came_ref, width - (2 - i) * lanes, lanes)


def dot(a, b):
    return jnp.dot(a, b, preferred_element_type=jnp.float32)


def part_kernel(
    came_ref,
    mine_ref,
    other_ref,
    query_hbm,
    pair_hbm,
    queries_ref,
    pairs_ref,
    spread_ref,
    weight_ref,
    sems,
):
    peers, steps, width = came_ref.shape
    features = weight_ref.shape[1]
    rows = queries_ref.shape[1]
    games = rows // steps
    block = peers * steps
    group_index = lax.axis_index("group")
    level = group_index // (SIDES * CORES)
    side, core = lax.rem(group_index // CORES, SIDES), lax.rem(group_index, CORES)
    head = level * KV_HEADS // (peers // CORES)
    pair_rows = features // (peers * SIDES)

    def columns(source, index):
        return source.at[:, pl.ds(pl.multiple_of(index * HEAD, HEAD), HEAD)]

    copies = fetch(
        [
            (columns(query_hbm, (level * SIDES + 0) * CORES + core), weight_ref.at[0]),
            (columns(query_hbm, (level * SIDES + 1) * CORES + core), weight_ref.at[1]),
            (columns(pair_hbm, core * KV_HEADS + head), weight_ref.at[2]),
        ],
        sems,
    )
    inputs = jnp.concatenate(
        [cells_of(came_ref, game * features, features) for game in range(games)], axis=0
    )
    spot = lax.broadcasted_iota(jnp.int32, (1, 2 * block), 1)
    feature = lax.broadcasted_iota(jnp.int32, (features, 2 * block), 0)
    peer, step = spot % block // steps, spot % steps
    offset = jnp.where(spot < block, step, step + steps)
    spreads = []
    for turn in range(SIDES):
        owner = (peer // CORES * SIDES + (side ^ turn)) * CORES + peer % CORES
        source = jnp.where(offset < pair_rows, owner * pair_rows + offset, -1)
        spread = (feature == source).astype(jnp.float32).astype(jnp.bfloat16)
        spreads.append(dot(inputs, spread).astype(jnp.bfloat16))
    spread_ref[...] = spreads[1]
    pairs = dot(spreads[0][:, :block], cells_of(came_ref, width - 2 * LANES, LANES))
    pairs = pairs + dot(spreads[0][:, block:], cells_of(came_ref, width - LANES, LANES))
    mine, other = mine_ref[...], other_ref[...]
    first = dot(inputs, jnp.where(side == 0, mine, other))
    second = dot(inputs, jnp.where(side == 0, other, mine))
    for copy in copies:
        copy.wait()

    def put(ref, i, sums):
        for game in range(games):
            ref[:, game * steps : (game + 1) * steps, i * HEAD : (i + 1) * HEAD] = sums[
                game * block : (game + 1) * block
            ].reshape(peers, steps, HEAD)

    put(queries_ref, 0, first + dot(inputs, weight_ref[0]))
    put(queries_ref, 1, second + dot(inputs, weight_ref[1]))
    put(pairs_ref, 0, pairs + dot(inputs, weight_ref[2]))


def whole_kernel(queries_ref, pairs_ref, spread_ref, other_ref, after1_ref, after2_ref, after3_ref, part_ref):
    peers, rows, wide = queries_ref.shape
    block = spread_ref.shape[1] // 2
    games = spread_ref.shape[0] // block
    steps = rows // games
    part_ref[:, :, :wide] = queries_ref[...]
    pairs = dot(spread_ref[:, :block], other_ref[0]) + dot(spread_ref[:, block:], other_ref[1])
    for game in range(games):
        band = slice(game * steps, (game + 1) * steps)
        part_ref[:, band, wide:] = pairs_ref[:, band, :] + pairs[
            game * block : (game + 1) * block
        ].reshape(peers, steps, HEAD)


def sum_kernel(parts_ref, keep_ref, give_ref):
    core = lax.rem(lax.axis_index("group"), CORES)
    sums = jnp.sum(parts_ref[...], axis=0)
    heads = [sums[:, i * HEAD : (i + 1) * HEAD] for i in range(3)]
    keep_ref[:, :HEAD] = jnp.where(core == 0, heads[0], heads[1]).astype(jnp.bfloat16)
    give_ref[:, :HEAD] = jnp.where(core == 0, heads[1], heads[0]).astype(jnp.bfloat16)
    keep_ref[:, HEAD:] = heads[2].astype(jnp.bfloat16)
    give_ref[:, HEAD:] = heads[2].astype(jnp.bfloat16)


def join_kernel(after_ref, *refs):
    shard_ref = refs[-1]
    for shift, piece_ref in enumerate(refs[:-1]):
        shard_ref[shift] = piece_ref[...]


def facts_kernel(after_ref, named_ref, came_ref, other_ref, placed_ref, ids_ref):
    peers, steps, width = came_ref.shape
    slots, rows = placed_ref.shape
    group_index = lax.axis_index("group")
    side = lax.rem(group_index // CORES, SIDES)
    capacity = slots // (peers * SIDES)

    named = named_ref[...].astype(jnp.float32)
    before = lax.broadcasted_iota(jnp.int32, (rows, rows), 0) < lax.broadcasted_iota(
        jnp.int32, (rows, rows), 1
    )
    rank = jnp.sum(jnp.where((column(named) == named) & before, 1.0, 0.0), axis=0, keepdims=True)
    slot = jnp.where(named >= 0, named * capacity + rank, -1.0)
    index = lax.broadcasted_iota(jnp.int32, (slots, rows), 0).astype(jnp.float32)
    placed_ref[...] = jnp.where(index == slot, 1.0, 0.0).astype(jnp.bfloat16)

    own = came_ref[:, :, width - LANES :].astype(jnp.float32)
    other = other_ref[1].astype(jnp.float32).reshape(own.shape)
    kind = lax.broadcasted_iota(jnp.int32, own.shape, 1) - (steps - 4)
    lane = lax.broadcasted_iota(jnp.int32, (peers, LANES), 1)
    out_lane = lax.broadcasted_iota(jnp.int32, (peers, slots), 1)
    out_peer = lax.broadcasted_iota(jnp.int32, (peers, slots), 0)
    ids = jnp.zeros((peers, slots), jnp.float32)
    for turn, facts in enumerate((own, other)):

        def pick(i):
            return jnp.sum(jnp.where(kind == i, facts, 0.0), axis=1)

        number = pick(0) * 4096.0 + pick(1) * 64.0 + pick(2)
        hit = (pick(3) == group_index.astype(jnp.float32)) & (lane < rows)
        coded = lane.astype(jnp.float32) * 262144.0 + number
        low = jnp.min(jnp.where(hit, coded, 1e9), axis=1, keepdims=True)
        high = jnp.max(jnp.where(hit, coded, -1.0), axis=1, keepdims=True)
        sender = (out_peer // CORES * SIDES + (side ^ turn)) * CORES + out_peer % CORES
        for k, (coded, there) in enumerate(((low, high >= 0), (high, high > low))):
            number = (coded.astype(jnp.int32) & 262143).astype(jnp.float32)
            value = jnp.where(there, number, -1.0)
            ids = ids + jnp.where(out_lane == sender * capacity + k, value, 0.0)
    ids_ref[...] = jnp.sum(ids, axis=0, keepdims=True).astype(jnp.int32)


def attend_kernel(
    lengths_ref,
    mine_ref,
    placed_ref,
    shard0_ref,
    shard1_ref,
    shard2_ref,
    shard3_ref,
    packed_ref,
):
    shards = (shard0_ref, shard1_ref, shard2_ref, shard3_ref)
    count, _, rounds, games, block, _ = shard0_ref.shape
    rows = mine_ref.shape[0]
    steps = rows // games
    heads = CORES
    n_tp = count * len(shards)
    factor = 1.0 / math.sqrt(HEAD)
    mine = mine_ref[...].astype(jnp.float32)
    first, second = mine[:, : 2 * HEAD], mine[:, 2 * HEAD :]
    even = lax.rem(lax.axis_index("tp"), 2) == 0
    with_keys, with_values = jnp.where(even, first, second), jnp.where(even, second, first)
    spot = lax.broadcasted_iota(jnp.int32, (1, count * rounds * block), 1)
    tp_index = lax.axis_index("tp")
    positions = []
    for shift in range(len(shards)):
        across = lax.rem(tp_index, len(shards)) ^ shift
        down = (tp_index // len(shards)) ^ (spot // (rounds * block))
        tp = down * len(shards) + across
        positions.append((spot // block % rounds * n_tp + tp) * block + spot % block)
    contract = (((1,), (1,)), ((), ()))
    games_out = []
    for game in range(games):
        bands = [x[game * steps : (game + 1) * steps] for x in (with_keys, with_values)]
        queries = jnp.concatenate([band[:, :HEAD] for band in bands], axis=0).astype(jnp.bfloat16)
        new_keys, new_values = [band[:, HEAD:].astype(jnp.bfloat16) for band in bands]
        new_scores = factor * lax.dot_general(
            queries, new_keys, contract, preferred_element_type=jnp.float32
        )
        later = lax.broadcasted_iota(jnp.int32, new_scores.shape, 1)
        step = lax.broadcasted_iota(jnp.int32, new_scores.shape, 0) % steps
        new_valid = later <= step
        top = jnp.max(jnp.where(new_valid, new_scores, NEG_FILL), axis=1, keepdims=True)
        kept = []
        for shard_ref, position in zip(shards, positions):
            keys = shard_ref[:, 0, :, game].reshape(count * rounds * block, HEAD)
            scores = factor * lax.dot_general(
                queries, keys, contract, preferred_element_type=jnp.float32
            )
            scores = jnp.where(position < lengths_ref[game], scores, NEG_FILL)
            top = jnp.maximum(top, jnp.max(scores, axis=1, keepdims=True))
            kept.append(scores)
        weight = jnp.where(new_valid, jnp.exp(new_scores - top), 0.0).astype(jnp.bfloat16)
        total = jnp.sum(weight.astype(jnp.float32), axis=1, keepdims=True)
        mixed = jnp.dot(weight, new_values, preferred_element_type=jnp.float32)
        for shard_ref, position, scores in zip(shards, positions, kept):
            values = shard_ref[:, 1, :, game].reshape(count * rounds * block, HEAD)
            weight = jnp.where(
                position < lengths_ref[game], jnp.exp(scores - top), 0.0
            ).astype(jnp.bfloat16)
            total = total + jnp.sum(weight.astype(jnp.float32), axis=1, keepdims=True)
            mixed = mixed + jnp.dot(weight, values, preferred_element_type=jnp.float32)
        out = mixed / total
        games_out.append(
            jnp.concatenate([out[h * steps : (h + 1) * steps] for h in range(heads)], axis=1)
        )
    attended = jnp.concatenate(games_out, axis=0).astype(jnp.bfloat16)
    packed = jnp.dot(placed_ref[...], attended, preferred_element_type=jnp.float32)
    packed_ref[...] = packed.reshape(packed_ref.shape).astype(jnp.bfloat16)


def per_device(
    hidden,
    query_weight,
    key_value_weight,
    query_codes,
    query_scales,
    key_value_codes,
    key_value_scales,
    key_cache,
    value_cache,
    lengths,
    counts,
    learner,
    token_ids,
):
    games, steps, features = hidden.shape
    rows = games * steps
    n_group = lax.axis_size("group")
    n_tp = lax.axis_size("tp")
    peers = n_group // SIDES
    across = n_tp // KV_HEADS
    near = [
        [g for g in range(n_group) if g // CORES % SIDES == side] for side in range(SIDES)
    ]
    turn = []
    for g in range(n_group):
        level, side, core = g // (SIDES * CORES), g // CORES % SIDES, g % CORES
        for t in range(n_tp):
            to = (t // CORES * SIDES + side) * CORES + t % CORES
            turn.append((g * n_tp + t, to * n_tp + level * CORES + core))
    wide = HEADS // n_tp * HEAD
    capacity = max(2, 2 * rows // n_group)
    rounds, _, _, block, _ = key_cache.shape
    pair_rows = key_value_codes.shape[1]
    bf16 = jnp.bfloat16

    def far(x):
        return pltpu.with_memory_space_constraint(x, pltpu.HBM)


    def along(x, axis, shift):
        return lax.ppermute(x, axis, [(i, i ^ shift) for i in range(lax.axis_size(axis))])

    operands = (
        counts.reshape(1, games),
        hidden,
        key_value_codes[0],
        key_value_scales[0].T,
        learner.transpose(0, 2, 1),
        token_ids,
    )
    load, named = pl.pallas_call(
        load_kernel,
        out_shape=[
            jax.ShapeDtypeStruct((peers, steps, games * features + 2 * LANES), bf16),
            jax.ShapeDtypeStruct((1, rows), jnp.int32),
        ],
        grid=(1,),
        in_specs=[whole(x.shape) for x in operands],
        out_specs=[whole((peers, steps, games * features + 2 * LANES)), whole((1, rows))],
        compiler_params=PARAMS,
        name="load",
    )(*[far(x) for x in operands])
    came = lax.all_to_all(
        load, "group", split_axis=0, concat_axis=0, tiled=True, axis_index_groups=near
    )

    piece = jax.ShapeDtypeStruct((2, rounds, games, block, HEAD), bf16)
    query_delta, *pieces = pl.pallas_call(
        pieces_kernel,
        out_shape=[jax.ShapeDtypeStruct(query_codes.shape, bf16)] + [piece] * KV_HEADS,
        in_specs=[HBM] * 4,
        out_specs=[VMEM] * (1 + KV_HEADS),
        scratch_shapes=[
            pltpu.VMEM(query_codes.shape, bf16),
            pltpu.VMEM((1, features), jnp.float32),
            pltpu.SemaphoreType.DMA((2,)),
            pltpu.SemaphoreType.DMA((2 * KV_HEADS,)),
        ],
        compiler_params=PARAMS,
        name="pieces",
    )(far(query_codes), far(query_scales.T), far(key_cache), far(value_cache))
    for shift in range(2, KV_HEADS):
        pieces[shift] = along(pieces[shift], "tp", shift * across)
    query_other = along(query_delta, "group", CORES)
    rows_all = peers * steps
    other, later = pl.pallas_call(
        swap_kernel,
        out_shape=[jax.ShapeDtypeStruct((2, rows_all, LANES), bf16), piece],
        in_specs=[VMEM] * 2,
        out_specs=[VMEM] * 2,
        compiler_params=PARAMS,
        name="swap",
    )(came, pieces[1])
    other = along(other, "group", CORES)
    pieces[1] = along(later, "tp", across)

    queries, pairs, spread = pl.pallas_call(
        part_kernel,
        out_shape=[
            jax.ShapeDtypeStruct((peers, rows, wide), jnp.float32),
            jax.ShapeDtypeStruct((peers, rows, HEAD), jnp.float32),
            jax.ShapeDtypeStruct((games * rows_all, 2 * rows_all), bf16),
        ],
        in_specs=[VMEM] * 3 + [HBM] * 2,
        out_specs=[VMEM] * 3,
        scratch_shapes=[
            pltpu.VMEM((3, features, HEAD), bf16),
            pltpu.SemaphoreType.DMA((3,)),
        ],
        compiler_params=PARAMS,
        name="part",
    )(came, query_delta, query_other, far(query_weight), far(key_value_weight))
    part = pl.pallas_call(
        whole_kernel,
        out_shape=jax.ShapeDtypeStruct((peers, rows, wide + HEAD), jnp.float32),
        in_specs=[VMEM] * 4 + [ANY] * 3,
        out_specs=VMEM,
        compiler_params=PARAMS,
        name="whole",
    )(queries, pairs, spread, other, *pieces[1:])
    parts = lax.all_to_all(part, "tp", split_axis=0, concat_axis=0, tiled=True)

    shard = pl.pallas_call(
        join_kernel,
        out_shape=jax.ShapeDtypeStruct((KV_HEADS,) + piece.shape, bf16),
        in_specs=[ANY] + [VMEM] * KV_HEADS,
        out_specs=VMEM,
        compiler_params=PARAMS,
        name="join",
    )(queries, *pieces)
    shards = [shard]
    for shift in range(1, across):
        shards.append(along(shard, "tp", shift))
    keep, give = pl.pallas_call(
        sum_kernel,
        out_shape=[jax.ShapeDtypeStruct((rows, 2 * HEAD), bf16)] * 2,
        in_specs=[VMEM],
        out_specs=[VMEM] * 2,
        compiler_params=PARAMS,
        name="sum",
    )(parts)
    got = along(give, "group", 1)
    mine = lax.ppermute(jnp.concatenate([keep, got], axis=1), ("group", "tp"), turn)

    placed, ids_back = pl.pallas_call(
        facts_kernel,
        out_shape=[
            jax.ShapeDtypeStruct((n_group * capacity, rows), bf16),
            jax.ShapeDtypeStruct((1, n_group * capacity), jnp.int32),
        ],
        in_specs=[ANY] + [VMEM] * 3,
        out_specs=[VMEM] * 2,
        compiler_params=PARAMS,
        name="facts",
    )(parts, named, came, other)

    packed = pl.pallas_call(
        attend_kernel,
        out_shape=jax.ShapeDtypeStruct((n_group, capacity, wide), bf16),
        in_specs=[SMEM] + [VMEM] * 6,
        out_specs=VMEM,
        compiler_params=PARAMS,
        name="attend",
    )(lengths, mine, placed, *shards)
    rows_back = lax.all_to_all(packed, "group", split_axis=0, concat_axis=1, tiled=True)
    return (rows_back, ids_back)


def solution(mesh):
    placed = (
        P("group", None, "tp"),
        P("tp", None),
        P("tp", None),
        P("tp", "group"),
        P("tp", "group"),
        P("tp", "group", None),
        P("tp", "group", None),
        P(None, "tp", "group", None, None),
        P(None, "tp", "group", None, None),
        P("group"),
        P("group"),
        P("group", None, None),
        P("group", None),
    )
    return jax.shard_map(
        per_device,
        mesh=mesh,
        in_specs=placed,
        out_specs=(P("group", None, "tp"), P("group", None)),
        check_vma=False,
    )
```
